128 devices in a mesh: seq: 64 (over y, z, x), head: 2 (over core).
Axes of the slice: x: 4, y: 4, z: 4, core: 2. Of those that a mesh axis runs over, the one named last changes fastest.
Arguments:
- image_qkv: bfloat16 [3, 7680, 2432], P(None, 'seq', 'head'), may hold values from -10 to 10
- text_qkv: bfloat16 [3, 512, 2432], P(None, 'seq', 'head'), may hold values from -5 to 5
- image_grad: bfloat16 [7680, 2432], P('seq', 'head'), may hold values from -6 to 6
- text_grad: bfloat16 [512, 2432], P('seq', 'head'), may hold values from -6 to 6
- text_len: int32 [1], replicated, may hold values from 64 to 512
Outputs:
- image_dqkv: bfloat16 [3, 7680, 2432], P(None, 'seq', 'head')
- text_dqkv: bfloat16 [3, 512, 2432], P(None, 'seq', 'head')
The draws below stay inside these ranges and needn't reach their ends.
All inputs are finite; a program needn't handle non-finite values.
Results may differ from the reference program's by a relative error of at most 0.0095.
Values may be sent and summed in bfloat16 or wider, within the bound.
A program may use at most 128 MiB of HBM per device.

```python
import jax
import jax.numpy as jnp
from jax import lax

HEADS = 38
HEAD_DIM = 64
WIDTH = 2432
IMAGE = 7680
TEXT = 512


def draw_image_qkv(key, part):
    key = jax.random.fold_in(key, 11)
    first = jax.random.fold_in(key, 0)
    base = jnp.clip(jax.random.normal(first, (3, IMAGE, WIDTH), jnp.float32), -5.0, 5.0)
    ramp = 0.6 + 1.2 * jnp.arange(IMAGE, dtype=jnp.float32) / IMAGE
    scaled = base.at[1].multiply(ramp[:, None])
    return scaled.astype(jnp.bfloat16)


def shard_levels(rng, dims, cuts, least, high):
    def one(axis_at, shards_of):
        heights = jax.random.uniform(jax.random.fold_in(jax.random.fold_in(rng, 6), axis_at), (shards_of,), jnp.float32, least / len(cuts), high / len(cuts))
        return jnp.repeat(jnp.exp(heights), dims[axis_at] // shards_of).reshape((-1,) + (1,) * (len(dims) - axis_at - 1))

    level = one(*cuts[0])
    for cut in cuts[1:]:
        level = level * one(*cut)
    return level


def bell_draw(stream_key, shape, deviation, most, cuts=(), kind=jnp.bfloat16):
    values = deviation * jax.random.normal(stream_key, shape, jnp.float32)
    if cuts:
        values = values * shard_levels(stream_key, shape, cuts, -0.22, 0.18)
    return jnp.clip(values, -most, most).astype(kind)


def setup_inputs(seed: int = 0) -> dict:
    seeds = jax.random.split(jax.random.key(seed), 6)
    image_qkv = draw_image_qkv(jax.random.fold_in(seeds[5], 71), 0)
    text_qkv = bell_draw(seeds[1], (3, TEXT, WIDTH), 1.0, 5.0, ((1, 64), (2, 2)))
    image_grad = bell_draw(seeds[2], (IMAGE, WIDTH), 1.0, 6.0, ((0, 64), (1, 2)))
    text_grad = bell_draw(seeds[3], (TEXT, WIDTH), 1.0, 6.0, ((0, 64), (1, 2)))
    text_len = jax.random.randint(seeds[4], (1,), TEXT // 8, TEXT + 1).astype(jnp.int32)
    return dict(image_qkv=image_qkv, text_qkv=text_qkv, image_grad=image_grad, text_grad=text_grad, text_len=text_len)


def reference(image_qkv, text_qkv, image_grad, text_grad, text_len):
    queries = jnp.concatenate([image_qkv[0], text_qkv[0]], 0)
    keys = jnp.concatenate([image_qkv[1], text_qkv[1]], 0)
    values = jnp.concatenate([image_qkv[2], text_qkv[2]], 0)
    grads = jnp.concatenate([image_grad, text_grad], 0)
    valid = jnp.concatenate([jnp.ones((IMAGE,), bool), jnp.arange(TEXT, dtype=jnp.int32) < text_len[0]], 0)
    scale = HEAD_DIM ** -0.5

    def per_head(index):
        start = (index * HEAD_DIM).astype(jnp.int32)
        query = lax.dynamic_slice_in_dim(queries, start, HEAD_DIM, 1)
        key_h = lax.dynamic_slice_in_dim(keys, start, HEAD_DIM, 1)
        value = lax.dynamic_slice_in_dim(values, start, HEAD_DIM, 1)
        grad = lax.dynamic_slice_in_dim(grads, start, HEAD_DIM, 1)
        scores = jnp.dot(query, key_h.T, preferred_element_type=jnp.float32) * scale
        scores = jnp.where(valid[None, :], scores, -jnp.inf)
        top = jnp.max(scores, 1, keepdims=True)
        lse = top + jnp.log(jnp.sum(jnp.exp(scores - top), 1, keepdims=True))
        probs = jnp.exp(scores - lse)
        dprobs = jnp.dot(grad, value.T, preferred_element_type=jnp.float32)
        delta = jnp.sum(probs * dprobs, 1, keepdims=True)
        grad_v = jnp.dot(probs.astype(jnp.bfloat16).T, grad, preferred_element_type=jnp.float32)
        dscore = (probs * (dprobs - delta) * scale).astype(jnp.bfloat16)
        grad_q = jnp.dot(dscore, key_h, preferred_element_type=jnp.float32)
        grad_k = jnp.dot(dscore.T, query, preferred_element_type=jnp.float32)
        return grad_q, grad_k, grad_v

    grad_q, grad_k, grad_v = lax.map(per_head, jnp.arange(HEADS, dtype=jnp.int32))
    total = IMAGE + TEXT

    def joined(block):
        return jnp.moveaxis(block, 0, 1).reshape(total, HEADS * HEAD_DIM)

    stacked = jnp.stack([joined(grad_q), joined(grad_k), joined(grad_v)])
    return stacked[:, :IMAGE].astype(jnp.bfloat16), stacked[:, IMAGE:].astype(jnp.bfloat16)
```

```python
import jax
import jax.numpy as jnp
from jax import lax
from jax.experimental import pallas as pl
from jax.experimental.pallas import tpu as pltpu
from jax.sharding import PartitionSpec as P

F32 = jnp.float32
BF = jnp.bfloat16
MESH = pl.DeviceIdType.MESH
NT = (((1,), (1,)), ((), ()))
NN = (((1,), (0,)), ((), ()))
HEAD_DIM = 64
SIDE = 4
HG = 5
TOK = 128
ROWS = SIDE * TOK
KEYS = SIDE * ROWS
SCALE = HEAD_DIM**-0.5
LOG = SCALE * 1.4426950408889634
NEG = -1e30
CHUNK = 256


def dot(a, b, dims):
    return lax.dot_general(a, b, dims, preferred_element_type=F32)


def kernel(
    tl_ref, qg_own, kv_own, out_ref,
    qg_all, kv_all, kt_all, s_ref, p_ref, dp_ref, ak, av, st,
    dq_st, dkv_st, rs_q, rs_kv, g_q, g_kv, f_q, f_kv,
    a_s, a_r, b_s, b_r, st_s, st_r, r_s, r_r, g_s, g_r,
):
    seq = lax.axis_index("seq")
    core = lax.axis_index("head")
    y, z, x = seq // 16, lax.rem(seq // 4, 4), lax.rem(seq, 4)

    def fwd(i, r):
        return lax.rem(i + r, SIDE)

    def back(i, r):
        return lax.rem(i + SIDE - r, SIDE)

    def at_x(i):
        return (y * 16 + z * 4 + i, core)

    def at_y(i):
        return (i * 16 + z * 4 + x, core)

    def at_z(i):
        return (y * 16 + i * 4 + x, core)

    def remote(src, dst, send, recv, device):
        return pltpu.make_async_remote_copy(
            src_ref=src, dst_ref=dst, send_sem=send, recv_sem=recv,
            device_id=device, device_id_type=MESH,
        )

    others = range(1, SIDE)

    def copies_a(h, r):
        t = fwd(x, r)
        return [
            remote(qg_own.at[HG * t + h], qg_all.at[h, y, x], a_s.at[0, h, r], a_r.at[0, h, r], at_x(t)),
            remote(kv_own.at[HG * t + h], kv_all.at[h, z, x], a_s.at[1, h, r], a_r.at[1, h, r], at_x(t)),
        ]

    def arrive_a(h, r):
        f = back(x, r)
        return [
            remote(qg_own.at[h], qg_all.at[h, y, f], a_s.at[0, h, r], a_r.at[0, h, r], at_x(f)),
            remote(kv_own.at[h], kv_all.at[h, z, f], a_s.at[1, h, r], a_r.at[1, h, r], at_x(f)),
        ]

    def copies_b(h, r):
        return [
            remote(qg_all.at[h, y], qg_all.at[h, y], b_s.at[0, h, r], b_r.at[0, h, r], at_y(fwd(y, r))),
            remote(kv_all.at[h, z], kv_all.at[h, z], b_s.at[1, h, r], b_r.at[1, h, r], at_z(fwd(z, r))),
        ]

    def arrive_b(h, r):
        fy, fz = back(y, r), back(z, r)
        return [
            remote(qg_all.at[h, fy], qg_all.at[h, fy], b_s.at[0, h, r], b_r.at[0, h, r], at_y(fy)),
            remote(kv_all.at[h, fz], kv_all.at[h, fz], b_s.at[1, h, r], b_r.at[1, h, r], at_z(fz)),
        ]

    def copy_st(u, r):
        return remote(st.at[u, 0], st.at[u, r], st_s.at[u, r], st_r.at[u, r], at_y(fwd(y, r)))

    def copy_rq(h, r):
        t = fwd(y, r)
        return remote(dq_st.at[h, t], rs_q.at[h, r - 1], r_s.at[0, h, r], r_r.at[0, h, r], at_y(t))

    def copy_rkv(h, r):
        t = fwd(z, r)
        return remote(dkv_st.at[h, t], rs_kv.at[h, r - 1], r_s.at[1, h, r], r_r.at[1, h, r], at_z(t))

    def copies_g(h, r):
        t = fwd(x, r)
        return [
            remote(g_q.at[h, t], f_q.at[HG * x + h], g_s.at[0, h, r], g_r.at[0, h, r], at_x(t)),
            remote(g_kv.at[h, t], f_kv.at[HG * x + h], g_s.at[1, h, r], g_r.at[1, h, r], at_x(t)),
        ]

    def arrive_g(h, r):
        f = back(x, r)
        return [
            remote(g_q.at[h, f], f_q.at[HG * f + h], g_s.at[0, h, r], g_r.at[0, h, r], at_x(f)),
            remote(g_kv.at[h, f], f_kv.at[HG * f + h], g_s.at[1, h, r], g_r.at[1, h, r], at_x(f)),
        ]

    barrier = pltpu.get_barrier_semaphore()
    for r in others:
        for place in (at_x(fwd(x, r)), at_y(fwd(y, r)), at_z(fwd(z, r))):
            pl.semaphore_signal(barrier, inc=1, device_id=place, device_id_type=MESH)
    pl.semaphore_wait(barrier, 3 * (SIDE - 1))

    def start_a(h, carry):
        for r in others:
            for copy in copies_a(h, r):
                copy.start()
        qg_all[h, y, x] = qg_own[HG * x + h]
        kv_all[h, z, x] = kv_own[HG * x + h]
        return carry

    lax.fori_loop(0, HG, start_a, 0)

    def spread(h):
        for r in others:
            for copy in arrive_a(h, r):
                copy.wait_recv()
        for r in others:
            for copy in copies_b(h, r):
                copy.start()

    def receive(h):
        for r in others:
            for copy in arrive_b(h, r):
                copy.wait_recv()
        for k in range(SIDE):
            kt_all[h, k] = kv_all[h, k].reshape(ROWS, TOK).T[:HEAD_DIM]

    def phase1(h, half):
        def block(j, carry):
            qg = qg_all[h, 2 * half + j].reshape(ROWS, TOK)
            lane = lax.broadcasted_iota(jnp.int32, qg.shape, 1)
            q0 = jnp.where(lane < HEAD_DIM, qg, jnp.zeros_like(qg))
            g0 = jnp.where(lane < HEAD_DIM, jnp.zeros_like(qg), qg)
            sub = lax.broadcasted_iota(jnp.int32, (8, ROWS), 0)
            top = jnp.full((8, ROWS), NEG, F32)
            for k in range(SIDE):
                s = dot(kv_all[h, k].reshape(ROWS, TOK), q0, NT)
                s_ref[k * ROWS : (k + 1) * ROWS, :] = s
                parts = s.reshape(SIDE, TOK // 8, 8, ROWS)
                top = jnp.maximum(top, jnp.max(parts[:, : TOK // 8 - 1].reshape(-1, 8, ROWS), axis=0))
                for i in range(SIDE):
                    valid = (y * 16 + k * 4 + i) * 8 + sub < tl_ref[0]
                    text = jnp.where(valid, parts[i, TOK // 8 - 1], NEG)
                    end = k * ROWS + (i + 1) * TOK
                    s_ref[end - 8 : end, :] = text
                    top = jnp.maximum(top, text)
            top = jnp.max(top, axis=0, keepdims=True) * LOG
            total = jnp.zeros((8, ROWS), F32)
            weighted = jnp.zeros((8, ROWS), F32)
            for k in range(SIDE):
                rows = slice(k * ROWS, (k + 1) * ROWS)
                d = dot(kv_all[h, k].reshape(ROWS, TOK), g0, NT)
                p = jnp.exp2(s_ref[rows, :] * LOG - top)
                total += jnp.sum(p.reshape(-1, 8, ROWS), axis=0)
                weighted += jnp.sum((p * d).reshape(-1, 8, ROWS), axis=0)
                p_ref[half, j, rows, :] = p.astype(BF)
                dp_ref[half, j, rows, :] = d
            st[2 * h + half, 0, j] = jnp.concatenate(
                [
                    top,
                    jnp.sum(total, axis=0, keepdims=True),
                    jnp.sum(weighted, axis=0, keepdims=True),
                    jnp.zeros((5, ROWS), F32),
                ],
                0,
            )
            return carry

        lax.fori_loop(0, 2, block, 0)
        for r in others:
            copy_st(2 * h + half, r).start()

    def phase2(h, half):
        u = 2 * h + half
        for r in others:
            copy_st(u, r).wait_recv()
        if half == 0:
            ak[...] = jnp.zeros_like(ak)
            av[...] = jnp.zeros_like(av)

        def block(j, carry):
            stats = [st[u, r, j] for r in range(SIDE)]
            tops = [s[0:1] for s in stats]
            top = jnp.maximum(jnp.maximum(tops[0], tops[1]), jnp.maximum(tops[2], tops[3]))
            parts = [jnp.exp2(t - top) for t in tops]
            total = sum(s[1:2] * e for s, e in zip(stats, parts))
            factor = parts[0] / total
            delta = sum(s[2:3] * e for s, e in zip(stats, parts)) / total
            qg = qg_all[h, 2 * half + j].reshape(ROWS, TOK)
            dq = jnp.zeros((HEAD_DIM, ROWS), F32)
            for c in range(KEYS // CHUNK):
                rows = slice(c * CHUNK, (c + 1) * CHUNK)
                p = p_ref[half, j, rows, :].astype(F32) * factor
                ds = (p * (dp_ref[half, j, rows, :] - delta)).astype(BF)
                av[rows, :] += dot(p.astype(BF), qg, NN)
                ak[rows, :] += dot(ds, qg, NN)
                per = ROWS // CHUNK
                part = c % per * CHUNK
                dq += dot(kt_all[h, c // per, :, part : part + CHUNK], ds, NN)
            dq_st[h, 2 * half + j] = (dq * SCALE).astype(BF)
            return carry

        lax.fori_loop(0, 2, block, 0)
        for r in others:
            t = fwd(y, r)

            @pl.when(t // 2 == half)
            def _():
                copy_rq(h, r).start()

        if half == 1:
            lane = lax.broadcasted_iota(jnp.int32, (ROWS, TOK), 1)
            for k in range(SIDE):
                rows = slice(k * ROWS, (k + 1) * ROWS)
                dkv_st[h, k] = jnp.where(lane < HEAD_DIM, ak[rows, :] * SCALE, av[rows, :]).astype(BF)
            for r in others:
                copy_rkv(h, r).start()

    def hand_over(h):
        for r in others:
            copy_rq(h, r).wait_recv()
            copy_rkv(h, r).wait_recv()
        dq = dq_st[h, y].astype(F32)
        dkv = dkv_st[h, z].astype(F32)
        for r in others:
            dq += rs_q[h, r - 1].astype(F32)
            dkv += rs_kv[h, r - 1].astype(F32)
        for i in range(SIDE):
            g_q[h, i] = dq[:, i * TOK : (i + 1) * TOK].astype(BF)
            g_kv[h, i] = dkv[i * TOK : (i + 1) * TOK, :].astype(BF)
        for r in others:
            for copy in copies_g(h, r):
                copy.start()
        f_q[HG * x + h] = g_q[h, x]
        f_kv[HG * x + h] = g_kv[h, x]

    spread(0)

    def step(h, carry):
        @pl.when(h < HG)
        def _():
            receive(h)
            phase1(h, 0)

        @pl.when(h < HG - 1)
        def _():
            spread(h + 1)

        @pl.when(h > 0)
        def _():
            phase2(h - 1, 1)

        @pl.when(h < HG)
        def _():
            phase1(h, 1)
            phase2(h, 0)

        @pl.when(h > 0)
        def _():
            hand_over(h - 1)

        return carry

    lax.fori_loop(0, HG + 1, step, 0)

    def finish(h, carry):
        for r in others:
            for copy in arrive_g(h, r):
                copy.wait_recv()
            for copy in copies_a(h, r) + copies_b(h, r) + copies_g(h, r):
                copy.wait_send()
            copy_rq(h, r).wait_send()
            copy_rkv(h, r).wait_send()
            copy_st(2 * h, r).wait_send()
            copy_st(2 * h + 1, r).wait_send()
        return carry

    lax.fori_loop(0, HG, finish, 0)

    for pair in range(SIDE * HG // 2):
        cols = slice(pair * TOK, (pair + 1) * TOK)
        first, second = f_kv[2 * pair].astype(F32), f_kv[2 * pair + 1].astype(F32)
        query = jnp.concatenate([f_q[2 * pair], f_q[2 * pair + 1]], 0).astype(F32)
        out_ref[0, :, cols] = query.T.astype(BF)
        out_ref[1, :, cols] = jnp.concatenate([first[:, :HEAD_DIM], second[:, :HEAD_DIM]], 1).astype(BF)
        out_ref[2, :, cols] = jnp.concatenate([first[:, HEAD_DIM:], second[:, HEAD_DIM:]], 1).astype(BF)


def body(image_qkv, text_qkv, image_grad, text_grad, text_len):
    image_rows = image_qkv.shape[1]
    width = image_qkv.shape[2]
    heads = width // HEAD_DIM
    slots = SIDE * HG

    def per_head(image, text):
        whole = jnp.concatenate([image, text], 0).reshape(TOK, heads, HEAD_DIM)
        return jnp.moveaxis(whole, 1, 0)

    query, key, value = (per_head(image_qkv[i], text_qkv[i]) for i in range(3))
    grad = per_head(image_grad, text_grad)
    pad = ((0, slots - heads), (0, 0), (0, 0))
    qg = jnp.pad(jnp.concatenate([query, grad], -1), pad)
    kv = jnp.pad(jnp.concatenate([key, value], -1), pad)
    vmem = pl.BlockSpec(memory_space=pltpu.VMEM)
    out = pl.pallas_call(
        kernel,
        out_shape=jax.ShapeDtypeStruct((3, TOK, slots * HEAD_DIM), BF),
        in_specs=[pl.BlockSpec(memory_space=pltpu.SMEM), vmem, vmem],
        out_specs=vmem,
        scratch_shapes=[
            pltpu.VMEM((HG, SIDE, SIDE, TOK, TOK), BF),
            pltpu.VMEM((HG, SIDE, SIDE, TOK, TOK), BF),
            pltpu.VMEM((HG, SIDE, HEAD_DIM, ROWS), BF),
            pltpu.VMEM((KEYS, ROWS), F32),
            pltpu.VMEM((2, 2, KEYS, ROWS), BF),
            pltpu.VMEM((2, 2, KEYS, ROWS), F32),
            pltpu.VMEM((KEYS, TOK), F32),
            pltpu.VMEM((KEYS, TOK), F32),
            pltpu.VMEM((2 * HG, SIDE, 2, 8, ROWS), F32),
            pltpu.VMEM((HG, SIDE, HEAD_DIM, ROWS), BF),
            pltpu.VMEM((HG, SIDE, ROWS, TOK), BF),
            pltpu.VMEM((HG, SIDE - 1, HEAD_DIM, ROWS), BF),
            pltpu.VMEM((HG, SIDE - 1, ROWS, TOK), BF),
            pltpu.VMEM((HG, SIDE, HEAD_DIM, TOK), BF),
            pltpu.VMEM((HG, SIDE, TOK, TOK), BF),
            pltpu.VMEM((slots, HEAD_DIM, TOK), BF),
            pltpu.VMEM((slots, TOK, TOK), BF),
        ]
        + [
            pltpu.SemaphoreType.DMA(shape)
            for shape in [(2, HG, SIDE)] * 4 + [(2 * HG, SIDE)] * 2 + [(2, HG, SIDE)] * 4
        ],
        compiler_params=pltpu.CompilerParams(
            collective_id=0, has_side_effects=True, vmem_limit_bytes=60 * 2**20
        ),
    )(text_len, qg, kv)
    return (out[:, :image_rows, :width], out[:, image_rows:, :width])


def solution(mesh):
    return jax.shard_map(
        body,
        mesh=mesh,
        in_specs=(
            P(None, "seq", "head"),
            P(None, "seq", "head"),
            P("seq", "head"),
            P("seq", "head"),
            P(),
        ),
        out_specs=(P(None, "seq", "head"), P(None, "seq", "head")),
        check_vma=False,
    )
```

```python
import jax
import jax.numpy as jnp
from jax import lax
from jax.experimental import pallas as pl
from jax.experimental.pallas import tpu as pltpu
from jax.sharding import PartitionSpec as P

F32 = jnp.float32
BF = jnp.bfloat16
MESH = pl.DeviceIdType.MESH
NT = (((1,), (1,)), ((), ()))
NN = (((1,), (0,)), ((), ()))
HEAD_DIM = 64
SIDE = 4
HG = 5
TOK = 128
ROWS = SIDE * TOK
KEYS = SIDE * ROWS
SCALE = HEAD_DIM**-0.5
LOG = SCALE * 1.4426950408889634
NEG = -1e30
CHUNK = 256


def dot(a, b, dims):
    return lax.dot_general(a, b, dims, preferred_element_type=F32)


def kernel(
    tl_ref, image_qkv, text_qkv, image_grad, text_grad, image_out, text_out,
    qg_own, kv_own, qg_all, kv_all, kt_all, s_ref, p_ref, dp_ref, ak, av, st,
    dq_st, dkv_st, r1_q, r1_kv, r2_q, r2_kv, g_q, g_kv, f_q, f_kv,
    a_s, a_r, b_s, b_r, st_s, st_r, r_s, r_r, g_s, g_r,
):
    seq = lax.axis_index("seq")
    core = lax.axis_index("head")
    y, z, x = seq // 16, lax.rem(seq // 4, 4), lax.rem(seq, 4)

    def fwd(i, r):
        return lax.rem(i + r, SIDE)

    def back(i, r):
        return lax.rem(i + SIDE - r, SIDE)

    def at_x(i):
        return (y * 16 + z * 4 + i, core)

    def at_y(i):
        return (i * 16 + z * 4 + x, core)

    def at_z(i):
        return (y * 16 + i * 4 + x, core)

    def remote(src, dst, send, recv, device):
        return pltpu.make_async_remote_copy(
            src_ref=src, dst_ref=dst, send_sem=send, recv_sem=recv,
            device_id=device, device_id_type=MESH,
        )

    others = range(1, SIDE)

    def copies_a(h, r):
        t = fwd(x, r)
        return [
            remote(qg_own.at[HG * t + h], qg_all.at[h, y, x], a_s.at[0, h, r], a_r.at[0, h, r], at_x(t)),
            remote(kv_own.at[HG * t + h], kv_all.at[h, z, x], a_s.at[1, h, r], a_r.at[1, h, r], at_x(t)),
        ]

    def arrive_a(h, r):
        f = back(x, r)
        return [
            remote(qg_own.at[h], qg_all.at[h, y, f], a_s.at[0, h, r], a_r.at[0, h, r], at_x(f)),
            remote(kv_own.at[h], kv_all.at[h, z, f], a_s.at[1, h, r], a_r.at[1, h, r], at_x(f)),
        ]

    def copies_b(h):
        yn, yp, zn, zp = fwd(y, 1), back(y, 1), fwd(z, 1), back(z, 1)
        return [
            remote(qg_all.at[h, y], qg_all.at[h, y], b_s.at[0, h, 0], b_r.at[0, h, 0], at_y(yn)),
            remote(kv_all.at[h, z], kv_all.at[h, z], b_s.at[1, h, 0], b_r.at[1, h, 0], at_z(zn)),
            remote(qg_all.at[h, y], qg_all.at[h, y], b_s.at[0, h, 1], b_r.at[0, h, 1], at_y(yp)),
            remote(kv_all.at[h, z], kv_all.at[h, z], b_s.at[1, h, 1], b_r.at[1, h, 1], at_z(zp)),
        ]

    def arrive_b(h):
        yn, yp, zn, zp = fwd(y, 1), back(y, 1), fwd(z, 1), back(z, 1)
        return [
            remote(qg_all.at[h, yp], qg_all.at[h, yp], b_s.at[0, h, 0], b_r.at[0, h, 0], at_y(yp)),
            remote(kv_all.at[h, zp], kv_all.at[h, zp], b_s.at[1, h, 0], b_r.at[1, h, 0], at_z(zp)),
            remote(qg_all.at[h, yn], qg_all.at[h, yn], b_s.at[0, h, 1], b_r.at[0, h, 1], at_y(yn)),
            remote(kv_all.at[h, zn], kv_all.at[h, zn], b_s.at[1, h, 1], b_r.at[1, h, 1], at_z(zn)),
        ]

    def relays(h, part, from_y, from_z, to_y, to_z):
        half = pl.ds(part * 2, 2)
        q = qg_all.at[h, from_y, half]
        k = kv_all.at[h, from_z, half]
        n = 2 + part
        return [
            remote(q, q, b_s.at[0, h, n], b_r.at[0, h, n], at_y(to_y)),
            remote(k, k, b_s.at[1, h, n], b_r.at[1, h, n], at_z(to_z)),
        ]

    def copies_f(h):
        yn, yp, zn, zp = fwd(y, 1), back(y, 1), fwd(z, 1), back(z, 1)
        return relays(h, 0, yp, zp, yn, zn) + relays(h, 1, yn, zn, yp, zp)

    def arrive_f(h):
        yn, yp, zn, zp = fwd(y, 1), back(y, 1), fwd(z, 1), back(z, 1)
        yo, zo = fwd(y, 2), fwd(z, 2)
        return relays(h, 0, yo, zo, yp, zp) + relays(h, 1, yo, zo, yn, zn)

    def copy_st(u, r):
        return remote(st.at[u, 0], st.at[u, r], st_s.at[u, r], st_r.at[u, r], at_y(fwd(y, r)))

    def copies_r1(h):
        yo, zo = fwd(y, 2), fwd(z, 2)
        places = ((at_y(fwd(y, 1)), at_z(fwd(z, 1))), (at_y(back(y, 1)), at_z(back(z, 1))))
        copies = []
        for n, (to_y, to_z) in enumerate(places):
            copies.append(remote(dq_st.at[h, yo, n], r1_q.at[h, n], r_s.at[0, h, n], r_r.at[0, h, n], to_y))
            copies.append(remote(dkv_st.at[h, zo, n], r1_kv.at[h, n], r_s.at[1, h, n], r_r.at[1, h, n], to_z))
        return copies

    def copies_r2(h):
        copies = []
        for n, (ty, tz) in enumerate(((fwd(y, 1), fwd(z, 1)), (back(y, 1), back(z, 1)))):
            k = 2 + n
            copies.append(remote(dq_st.at[h, ty], r2_q.at[h, n], r_s.at[0, h, k], r_r.at[0, h, k], at_y(ty)))
            copies.append(remote(dkv_st.at[h, tz], r2_kv.at[h, n], r_s.at[1, h, k], r_r.at[1, h, k], at_z(tz)))
        return copies

    def copies_g(h, r):
        t = fwd(x, r)
        return [
            remote(g_q.at[h, t], f_q.at[HG * x + h], g_s.at[0, h, r], g_r.at[0, h, r], at_x(t)),
            remote(g_kv.at[h, t], f_kv.at[HG * x + h], g_s.at[1, h, r], g_r.at[1, h, r], at_x(t)),
        ]

    def arrive_g(h, r):
        f = back(x, r)
        return [
            remote(g_q.at[h, f], f_q.at[HG * f + h], g_s.at[0, h, r], g_r.at[0, h, r], at_x(f)),
            remote(g_kv.at[h, f], f_kv.at[HG * f + h], g_s.at[1, h, r], g_r.at[1, h, r], at_x(f)),
        ]

    barrier = pltpu.get_barrier_semaphore()
    for r in others:
        for place in (at_x(fwd(x, r)), at_y(fwd(y, r)), at_z(fwd(z, r))):
            pl.semaphore_signal(barrier, inc=1, device_id=place, device_id_type=MESH)

    def column(image, text, pair):
        cols = slice(pair * TOK, min((pair + 1) * TOK, image.shape[-1]))
        return jnp.concatenate([image[:, cols].astype(F32), text[:, cols].astype(F32)], 0)

    heads = image_grad.shape[1] // HEAD_DIM
    for pair in range((heads + 1) // 2):
        query, key, value = (column(image_qkv.at[i], text_qkv.at[i], pair) for i in range(3))
        grad = column(image_grad, text_grad, pair)
        for own, left, right in ((qg_own, query, grad), (kv_own, key, value)):
            own[2 * pair] = jnp.concatenate([left[:, :HEAD_DIM], right[:, :HEAD_DIM]], 1).astype(BF)
            if 2 * pair + 1 < heads:
                own[2 * pair + 1] = jnp.concatenate([left[:, HEAD_DIM:], right[:, HEAD_DIM:]], 1).astype(BF)
    for slot in range(heads, SIDE * HG):
        qg_own[slot] = jnp.zeros((TOK, TOK), BF)
        kv_own[slot] = jnp.zeros((TOK, TOK), BF)

    pl.semaphore_wait(barrier, 3 * (SIDE - 1))

    def start_a(h):
        for r in others:
            for copy in copies_a(h, r):
                copy.start()
        qg_all[h, y, x] = qg_own[HG * x + h]
        kv_all[h, z, x] = kv_own[HG * x + h]

    def spread(h):
        for r in others:
            for copy in arrive_a(h, r):
                copy.wait_recv()
        for copy in copies_b(h):
            copy.start()

    def forward(h):
        for copy in arrive_b(h):
            copy.wait_recv()
        for copy in copies_f(h):
            copy.start()

    def receive(h):
        for copy in arrive_f(h):
            copy.wait_recv()
        for k in range(SIDE):
            kt_all[h, k] = kv_all[h, k].reshape(ROWS, TOK).T[:HEAD_DIM]

    def phase1(h, half):
        def block(j, carry):
            qg = qg_all[h, 2 * half + j].reshape(ROWS, TOK)
            lane = lax.broadcasted_iota(jnp.int32, qg.shape, 1)
            q0 = jnp.where(lane < HEAD_DIM, qg, jnp.zeros_like(qg))
            g0 = jnp.where(lane < HEAD_DIM, jnp.zeros_like(qg), qg)
            sub = lax.broadcasted_iota(jnp.int32, (8, ROWS), 0)
            top = jnp.full((8, ROWS), NEG, F32)
            for k in range(SIDE):
                s = dot(kv_all[h, k].reshape(ROWS, TOK), q0, NT)
                s_ref[k * ROWS : (k + 1) * ROWS, :] = s
                parts = s.reshape(SIDE, TOK // 8, 8, ROWS)
                top = jnp.maximum(top, jnp.max(parts[:, : TOK // 8 - 1].reshape(-1, 8, ROWS), axis=0))
                for i in range(SIDE):
                    valid = (y * 16 + k * 4 + i) * 8 + sub < tl_ref[0]
                    text = jnp.where(valid, parts[i, TOK // 8 - 1], NEG)
                    end = k * ROWS + (i + 1) * TOK
                    s_ref[end - 8 : end, :] = text
                    top = jnp.maximum(top, text)
            top = jnp.max(top, axis=0, keepdims=True) * LOG
            total = jnp.zeros((8, ROWS), F32)
            weighted = jnp.zeros((8, ROWS), F32)
            for k in range(SIDE):
                rows = slice(k * ROWS, (k + 1) * ROWS)
                d = dot(kv_all[h, k].reshape(ROWS, TOK), g0, NT)
                p = jnp.exp2(s_ref[rows, :] * LOG - top)
                total += jnp.sum(p.reshape(-1, 8, ROWS), axis=0)
                weighted += jnp.sum((p * d).reshape(-1, 8, ROWS), axis=0)
                p_ref[half, j, rows, :] = p.astype(BF)
                dp_ref[half, j, rows, :] = d
            stats = (top, jnp.sum(total, axis=0, keepdims=True), jnp.sum(weighted, axis=0, keepdims=True))
            parts = [s[:, i * TOK : (i + 1) * TOK] for s in stats for i in range(SIDE)]
            st[2 * h + half, 0, j] = jnp.concatenate(parts + [jnp.zeros((SIDE, TOK), F32)], 0)
            return carry

        lax.fori_loop(0, 2, block, 0)
        for r in others:
            copy_st(2 * h + half, r).start()

    def phase2(h, half):
        u = 2 * h + half
        for r in others:
            copy_st(u, r).wait_recv()
        if half == 0:
            ak[...] = jnp.zeros_like(ak)
            av[...] = jnp.zeros_like(av)

        def block(j, carry):
            stats = [st[u, r, j] for r in range(SIDE)]
            tops = [s[0:4] for s in stats]
            top = jnp.maximum(jnp.maximum(tops[0], tops[1]), jnp.maximum(tops[2], tops[3]))
            parts = [jnp.exp2(t - top) for t in tops]
            total = sum(s[4:8] * e for s, e in zip(stats, parts))
            factor = parts[0] / total
            delta = sum(s[8:12] * e for s, e in zip(stats, parts)) / total
            factor, delta = (
                jnp.concatenate([v[i : i + 1] for i in range(SIDE)], 1) for v in (factor, delta)
            )
            qg = qg_all[h, 2 * half + j].reshape(ROWS, TOK)
            dq = jnp.zeros((HEAD_DIM, ROWS), F32)
            for c in range(KEYS // CHUNK):
                rows = slice(c * CHUNK, (c + 1) * CHUNK)
                p = p_ref[half, j, rows, :].astype(F32) * factor
                ds = (p * (dp_ref[half, j, rows, :] - delta)).astype(BF)
                av[rows, :] += dot(p.astype(BF), qg, NN)
                ak[rows, :] += dot(ds, qg, NN)
                per = ROWS // CHUNK
                part = c % per * CHUNK
                dq += dot(kt_all[h, c // per, :, part : part + CHUNK], ds, NN)
            dq = (dq * SCALE).astype(BF)
            for i in range(2):
                dq_st[h, 2 * half + j, i] = dq[:, i * ROWS // 2 : (i + 1) * ROWS // 2]
            return carry

        lax.fori_loop(0, 2, block, 0)
        if half == 1:
            lane = lax.broadcasted_iota(jnp.int32, (ROWS, TOK), 1)
            for k in range(SIDE):
                rows = slice(k * ROWS, (k + 1) * ROWS)
                dkv = jnp.where(lane < HEAD_DIM, ak[rows, :] * SCALE, av[rows, :]).astype(BF)
                dkv_st[h, k] = dkv.reshape(2, ROWS // 2, TOK)
            for copy in copies_r1(h):
                copy.start()

    def combine(h):
        for copy in copies_r1(h):
            copy.wait_recv()
        for n, (ty, tz) in enumerate(((fwd(y, 1), fwd(z, 1)), (back(y, 1), back(z, 1)))):
            dq_st[h, ty, n] = (dq_st[h, ty, n].astype(F32) + r1_q[h, n].astype(F32)).astype(BF)
            dkv_st[h, tz, n] = (dkv_st[h, tz, n].astype(F32) + r1_kv[h, n].astype(F32)).astype(BF)
        for copy in copies_r2(h):
            copy.start()

    def hand_over(h):
        for copy in copies_r2(h):
            copy.wait_recv()
        for i in range(2):
            dq = dq_st[h, y, i].astype(F32) + r2_q[h, 0, i].astype(F32) + r2_q[h, 1, i].astype(F32)
            dkv = dkv_st[h, z, i].astype(F32) + r2_kv[h, 0, i].astype(F32) + r2_kv[h, 1, i].astype(F32)
            for k in range(2):
                g_q[h, 2 * i + k] = dq[:, k * TOK : (k + 1) * TOK].astype(BF)
                g_kv[h, 2 * i + k] = dkv[k * TOK : (k + 1) * TOK, :].astype(BF)
        for r in others:
            for copy in copies_g(h, r):
                copy.start()
        f_q[HG * x + h] = g_q[h, x]
        f_kv[HG * x + h] = g_kv[h, x]

    start_a(0)
    spread(0)
    start_a(1)
    forward(0)

    def step(h, carry):
        @pl.when(h < HG)
        def _():
            receive(h)

        @pl.when(h < HG - 2)
        def _():
            start_a(h + 2)

        @pl.when(h < HG)
        def _():
            phase1(h, 0)

        @pl.when(h < HG - 1)
        def _():
            spread(h + 1)

        @pl.when(h > 0)
        def _():
            phase2(h - 1, 1)

        @pl.when(h < HG)
        def _():
            phase1(h, 1)

        @pl.when(h < HG - 1)
        def _():
            forward(h + 1)

        @pl.when(h > 0)
        def _():
            combine(h - 1)

        @pl.when(h < HG)
        def _():
            phase2(h, 0)

        @pl.when(h > 0)
        def _():
            hand_over(h - 1)

        return carry

    lax.fori_loop(0, HG + 1, step, 0)

    def finish(h, carry):
        for r in others:
            for copy in arrive_g(h, r):
                copy.wait_recv()
            for copy in copies_a(h, r) + copies_g(h, r):
                copy.wait_send()
            copy_st(2 * h, r).wait_send()
            copy_st(2 * h + 1, r).wait_send()
        for copy in copies_b(h) + copies_f(h) + copies_r1(h) + copies_r2(h):
            copy.wait_send()
        return carry

    lax.fori_loop(0, HG, finish, 0)

    image_rows = image_grad.shape[0]
    for pair in range((heads + 1) // 2):
        both = 2 * pair + 1 < heads
        width = TOK if both else HEAD_DIM
        cols = slice(pair * TOK, pair * TOK + width)
        first, second = f_kv[2 * pair].astype(F32), f_kv[2 * pair + 1].astype(F32)
        query = jnp.concatenate([f_q[2 * pair], f_q[2 * pair + 1]], 0).astype(F32).T
        key = jnp.concatenate([first[:, :HEAD_DIM], second[:, :HEAD_DIM]], 1)
        value = jnp.concatenate([first[:, HEAD_DIM:], second[:, HEAD_DIM:]], 1)
        for i, whole in enumerate((query, key, value)):
            image_out[i, :, cols] = whole[:image_rows, :width].astype(BF)
            text_out[i, :, cols] = whole[image_rows:, :width].astype(BF)


def body(image_qkv, text_qkv, image_grad, text_grad, text_len):
    slots = SIDE * HG
    vmem = pl.BlockSpec(memory_space=pltpu.VMEM)
    return pl.pallas_call(
        kernel,
        out_shape=(
            jax.ShapeDtypeStruct(image_qkv.shape, BF),
            jax.ShapeDtypeStruct(text_qkv.shape, BF),
        ),
        in_specs=[pl.BlockSpec(memory_space=pltpu.SMEM), vmem, vmem, vmem, vmem],
        out_specs=(vmem, vmem),
        scratch_shapes=[
            pltpu.VMEM((slots, TOK, TOK), BF),
            pltpu.VMEM((slots, TOK, TOK), BF),
            pltpu.VMEM((HG, SIDE, SIDE, TOK, TOK), BF),
            pltpu.VMEM((HG, SIDE, SIDE, TOK, TOK), BF),
            pltpu.VMEM((HG, SIDE, HEAD_DIM, ROWS), BF),
            pltpu.VMEM((KEYS, ROWS), F32),
            pltpu.VMEM((2, 2, KEYS, ROWS), BF),
            pltpu.VMEM((2, 2, KEYS, ROWS), F32),
            pltpu.VMEM((KEYS, TOK), F32),
            pltpu.VMEM((KEYS, TOK), F32),
            pltpu.VMEM((2 * HG, SIDE, 2, 16, TOK), F32),
            pltpu.VMEM((HG, SIDE, 2, HEAD_DIM, ROWS // 2), BF),
            pltpu.VMEM((HG, SIDE, 2, ROWS // 2, TOK), BF),
            pltpu.VMEM((HG, 2, HEAD_DIM, ROWS // 2), BF),
            pltpu.VMEM((HG, 2, ROWS // 2, TOK), BF),
            pltpu.VMEM((HG, 2, 2, HEAD_DIM, ROWS // 2), BF),
            pltpu.VMEM((HG, 2, 2, ROWS // 2, TOK), BF),
            pltpu.VMEM((HG, SIDE, HEAD_DIM, TOK), BF),
            pltpu.VMEM((HG, SIDE, TOK, TOK), BF),
            pltpu.VMEM((slots, HEAD_DIM, TOK), BF),
            pltpu.VMEM((slots, TOK, TOK), BF),
        ]
        + [
            pltpu.SemaphoreType.DMA(shape)
            for shape in [(2, HG, SIDE)] * 4 + [(2 * HG, SIDE)] * 2 + [(2, HG, SIDE)] * 4
        ],
        compiler_params=pltpu.CompilerParams(
            collective_id=0, has_side_effects=True, vmem_limit_bytes=60 * 2**20
        ),
    )(text_len, image_qkv, text_qkv, image_grad, text_grad)


def solution(mesh):
    return jax.shard_map(
        body,
        mesh=mesh,
        in_specs=(
            P(None, "seq", "head"),
            P(None, "seq", "head"),
            P("seq", "head"),
            P("seq", "head"),
            P(),
        ),
        out_specs=(P(None, "seq", "head"), P(None, "seq", "head")),
        check_vma=False,
    )
```

```python
import jax
import jax.numpy as jnp
from jax import lax
from jax.experimental import pallas as pl
from jax.experimental.pallas import tpu as pltpu
from jax.sharding import PartitionSpec as P

F32 = jnp.float32
BF = jnp.bfloat16
MESH = pl.DeviceIdType.MESH
NT = (((1,), (1,)), ((), ()))
NN = (((1,), (0,)), ((), ()))
HEAD_DIM = 64
SIDE = 4
HG = 5
TOK = 128
ROWS = SIDE * TOK
KEYS = SIDE * ROWS
SCALE = HEAD_DIM**-0.5
LOG = SCALE * 1.4426950408889634
NEG = -1e30
CHUNK = 256


def dot(a, b, dims):
    return lax.dot_general(a, b, dims, preferred_element_type=F32)


def kernel(
    tl_ref, image_qkv, text_qkv, image_grad, text_grad, image_out, text_out,
    qg_own, kv_own, qg_all, kv_all, kt_all, s_ref, p_ref, dp_ref, acc, st,
    dq_st, dkv_st, r1_q, r1_kv, r2_q, r2_kv, g_q, g_kv, f_q, f_kv,
    a_s, a_r, b_s, b_r, st_s, st_r, r_s, r_r, g_s, g_r,
):
    seq = lax.axis_index("seq")
    core = lax.axis_index("head")
    y, z, x = seq // 16, lax.rem(seq // 4, 4), lax.rem(seq, 4)

    def fwd(i, r):
        return lax.rem(i + r, SIDE)

    def back(i, r):
        return lax.rem(i + SIDE - r, SIDE)

    def at_x(i):
        return (y * 16 + z * 4 + i, core)

    def at_y(i):
        return (i * 16 + z * 4 + x, core)

    def at_z(i):
        return (y * 16 + i * 4 + x, core)

    def remote(src, dst, send, recv, device):
        return pltpu.make_async_remote_copy(
            src_ref=src, dst_ref=dst, send_sem=send, recv_sem=recv,
            device_id=device, device_id_type=MESH,
        )

    others = range(1, SIDE)

    def copies_a(h, r):
        t = fwd(x, r)
        return [
            remote(qg_own.at[HG * t + h], qg_all.at[h, y, x], a_s.at[0, h, r], a_r.at[0, h, r], at_x(t)),
            remote(kv_own.at[HG * t + h], kv_all.at[h, z, x], a_s.at[1, h, r], a_r.at[1, h, r], at_x(t)),
        ]

    def arrive_a(h, r):
        f = back(x, r)
        return [
            remote(qg_own.at[h], qg_all.at[h, y, f], a_s.at[0, h, r], a_r.at[0, h, r], at_x(f)),
            remote(kv_own.at[h], kv_all.at[h, z, f], a_s.at[1, h, r], a_r.at[1, h, r], at_x(f)),
        ]

    def move(arr, h, block, r, way, to, halves):
        ref = (qg_all, kv_all)[arr].at[h, block, back(x, r)]
        n = SIDE * (way + 2 * halves) + r
        return remote(ref, ref, b_s.at[arr, h, n], b_r.at[arr, h, n], (at_y, at_z)[arr](to))

    def copies_b(h, r):
        return [move(a, h, i, r, w, (fwd, back)[w](i, 1), 0) for w in range(2) for a, i in enumerate((y, z))]

    def arrive_b(h, r):
        sides = [(a, w, (back, fwd)[w](i, 1)) for w in range(2) for a, i in enumerate((y, z))]
        return [move(a, h, f, r, w, f, 0) for a, w, f in sides]

    def copies_f(h, r):
        w = r % 2
        sides = [(a, (back, fwd)[w](i, 1), (fwd, back)[w](i, 1)) for a, i in enumerate((y, z))]
        return [move(a, h, f, r, w, t, 1) for a, f, t in sides]

    def arrive_f(h, r):
        w = r % 2
        sides = [(a, fwd(i, 2), (back, fwd)[w](i, 1)) for a, i in enumerate((y, z))]
        return [move(a, h, f, r, w, t, 1) for a, f, t in sides]

    def copy_st(u, r):
        return remote(st.at[u, 0], st.at[u, r], st_s.at[u, r], st_r.at[u, r], at_y(fwd(y, r)))

    def copies_r1(h):
        yo, zo = fwd(y, 2), fwd(z, 2)
        places = ((at_y(fwd(y, 1)), at_z(fwd(z, 1))), (at_y(back(y, 1)), at_z(back(z, 1))))
        copies = []
        for n, (to_y, to_z) in enumerate(places):
            copies.append(remote(dq_st.at[h, yo, n], r1_q.at[h, n], r_s.at[0, h, n], r_r.at[0, h, n], to_y))
            copies.append(remote(dkv_st.at[h, zo, n], r1_kv.at[h, n], r_s.at[1, h, n], r_r.at[1, h, n], to_z))
        return copies

    def copies_r2(h):
        copies = []
        for n, (ty, tz) in enumerate(((fwd(y, 1), fwd(z, 1)), (back(y, 1), back(z, 1)))):
            k = 2 + n
            copies.append(remote(dq_st.at[h, ty], r2_q.at[h, n], r_s.at[0, h, k], r_r.at[0, h, k], at_y(ty)))
            copies.append(remote(dkv_st.at[h, tz], r2_kv.at[h, n], r_s.at[1, h, k], r_r.at[1, h, k], at_z(tz)))
        return copies

    def copies_g(h, r):
        t = fwd(x, r)
        return [
            remote(g_q.at[h, t], f_q.at[HG * x + h], g_s.at[0, h, r], g_r.at[0, h, r], at_x(t)),
            remote(g_kv.at[h, t], f_kv.at[HG * x + h], g_s.at[1, h, r], g_r.at[1, h, r], at_x(t)),
        ]

    def arrive_g(h, r):
        f = back(x, r)
        return [
            remote(g_q.at[h, f], f_q.at[HG * f + h], g_s.at[0, h, r], g_r.at[0, h, r], at_x(f)),
            remote(g_kv.at[h, f], f_kv.at[HG * f + h], g_s.at[1, h, r], g_r.at[1, h, r], at_x(f)),
        ]

    barrier = pltpu.get_barrier_semaphore()
    for r in others:
        for place in (at_x(fwd(x, r)), at_y(fwd(y, r)), at_z(fwd(z, r))):
            pl.semaphore_signal(barrier, inc=1, device_id=place, device_id_type=MESH)

    def column(image, text, pair):
        cols = slice(pair * TOK, min((pair + 1) * TOK, image.shape[-1]))
        return jnp.concatenate([image[:, cols].astype(F32), text[:, cols].astype(F32)], 0)

    heads = image_grad.shape[1] // HEAD_DIM
    for pair in range((heads + 1) // 2):
        query, key, value = (column(image_qkv.at[i], text_qkv.at[i], pair) for i in range(3))
        grad = column(image_grad, text_grad, pair)
        for own, left, right in ((qg_own, query, grad), (kv_own, key, value)):
            own[2 * pair] = jnp.concatenate([left[:, :HEAD_DIM], right[:, :HEAD_DIM]], 1).astype(BF)
            if 2 * pair + 1 < heads:
                own[2 * pair + 1] = jnp.concatenate([left[:, HEAD_DIM:], right[:, HEAD_DIM:]], 1).astype(BF)
    for slot in range(heads, SIDE * HG):
        qg_own[slot] = jnp.zeros((TOK, TOK), BF)
        kv_own[slot] = jnp.zeros((TOK, TOK), BF)

    pl.semaphore_wait(barrier, 3 * (SIDE - 1))

    def start_a(h):
        for r in others:
            for copy in copies_a(h, r):
                copy.start()
        qg_all[h, y, x] = qg_own[HG * x + h]
        kv_all[h, z, x] = kv_own[HG * x + h]

    order = (0, 1, 3, 2)

    def spread(h):
        for r in order:
            if r:
                for copy in arrive_a(h, r):
                    copy.wait_recv()
            for copy in copies_b(h, r):
                copy.start()

    def forward(h):
        for r in order:
            for copy in arrive_b(h, r):
                copy.wait_recv()
            for copy in copies_f(h, r):
                copy.start()

    def receive(h):
        for r in order:
            for copy in arrive_f(h, r):
                copy.wait_recv()
        for k in range(SIDE):
            kt_all[h, k] = kv_all[h, k].reshape(ROWS, TOK).T[:HEAD_DIM]

    def phase1(h, half):
        count = 2 * ROWS
        qg = qg_all[h, 2 * half : 2 * half + 2].reshape(count, TOK)
        lane = lax.broadcasted_iota(jnp.int32, qg.shape, 1)
        q0 = jnp.where(lane < HEAD_DIM, qg, jnp.zeros_like(qg))
        g0 = jnp.where(lane < HEAD_DIM, jnp.zeros_like(qg), qg)
        sub = lax.broadcasted_iota(jnp.int32, (8, count), 0)
        top = jnp.full((8, count), NEG, F32)
        for k in range(SIDE):
            s = dot(kv_all[h, k].reshape(ROWS, TOK), q0, NT)
            s_ref[k * ROWS : (k + 1) * ROWS, :] = s
            parts = s.reshape(SIDE, TOK // 8, 8, count)
            top = jnp.maximum(top, jnp.max(parts[:, : TOK // 8 - 1].reshape(-1, 8, count), axis=0))
            for i in range(SIDE):
                valid = (y * 16 + k * 4 + i) * 8 + sub < tl_ref[0]
                text = jnp.where(valid, parts[i, TOK // 8 - 1], NEG)
                end = k * ROWS + (i + 1) * TOK
                s_ref[end - 8 : end, :] = text
                top = jnp.maximum(top, text)
        top = jnp.max(top, axis=0, keepdims=True) * LOG
        total = jnp.zeros((8, count), F32)
        weighted = jnp.zeros((8, count), F32)
        for k in range(SIDE):
            rows = slice(k * ROWS, (k + 1) * ROWS)
            d = dot(kv_all[h, k].reshape(ROWS, TOK), g0, NT)
            p = jnp.exp2(s_ref[rows, :] * LOG - top)
            total += jnp.sum(p.reshape(-1, 8, count), axis=0)
            weighted += jnp.sum((p * d).reshape(-1, 8, count), axis=0)
            p_ref[half, rows, :] = p.astype(BF)
            dp_ref[half, rows, :] = d
        stats = (top, jnp.sum(total, axis=0, keepdims=True), jnp.sum(weighted, axis=0, keepdims=True))
        parts = [s[:, i * TOK : (i + 1) * TOK] for s in stats for i in range(2 * SIDE)]
        st[2 * h + half, 0] = jnp.concatenate(parts, 0)
        for r in others:
            copy_st(2 * h + half, r).start()

    def phase2(h, half):
        u = 2 * h + half
        for r in others:
            copy_st(u, r).wait_recv()
        stats = [st[u, r] for r in range(SIDE)]
        tops = [s[0:8] for s in stats]
        top = jnp.maximum(jnp.maximum(tops[0], tops[1]), jnp.maximum(tops[2], tops[3]))
        parts = [jnp.exp2(t - top) for t in tops]
        total = sum(s[8:16] * e for s, e in zip(stats, parts))
        factors = parts[0] / total
        deltas = sum(s[16:24] * e for s, e in zip(stats, parts)) / total
        for j in range(2):
            factor, delta = (
                jnp.concatenate([v[i : i + 1] for i in range(SIDE * j, SIDE * (j + 1))], 1)
                for v in (factors, deltas)
            )
            qg = qg_all[h, 2 * half + j].reshape(ROWS, TOK)
            lane = lax.broadcasted_iota(jnp.int32, qg.shape, 1)
            q0 = jnp.where(lane < HEAD_DIM, qg, jnp.zeros_like(qg))
            g0 = jnp.where(lane < HEAD_DIM, jnp.zeros_like(qg), qg)
            cols = slice(j * ROWS, (j + 1) * ROWS)
            dq = jnp.zeros((HEAD_DIM, ROWS), F32)
            for c in range(KEYS // CHUNK):
                rows = slice(c * CHUNK, (c + 1) * CHUNK)
                p = p_ref[half, rows, cols].astype(F32) * factor
                ds = (p * (dp_ref[half, rows, cols] - delta)).astype(BF)
                part = dot(p.astype(BF), g0, NN) + dot(ds, q0, NN)
                if half == 0 and j == 0:
                    acc[rows, :] = part
                else:
                    acc[rows, :] += part
                per = ROWS // CHUNK
                at = c % per * CHUNK
                dq += dot(kt_all[h, c // per, :, at : at + CHUNK], ds, NN)
            dq = (dq * SCALE).astype(BF)
            for i in range(2):
                dq_st[h, 2 * half + j, i] = dq[:, i * ROWS // 2 : (i + 1) * ROWS // 2]
        if half == 1:
            lane = lax.broadcasted_iota(jnp.int32, (ROWS, TOK), 1)
            for k in range(SIDE):
                rows = slice(k * ROWS, (k + 1) * ROWS)
                dkv = (acc[rows, :] * jnp.where(lane < HEAD_DIM, SCALE, 1.0)).astype(BF)
                dkv_st[h, k] = dkv.reshape(2, ROWS // 2, TOK)
            for copy in copies_r1(h):
                copy.start()

    def combine(h):
        for copy in copies_r1(h):
            copy.wait_recv()
        for n, (ty, tz) in enumerate(((fwd(y, 1), fwd(z, 1)), (back(y, 1), back(z, 1)))):
            dq_st[h, ty, n] = (dq_st[h, ty, n].astype(F32) + r1_q[h, n].astype(F32)).astype(BF)
            dkv_st[h, tz, n] = (dkv_st[h, tz, n].astype(F32) + r1_kv[h, n].astype(F32)).astype(BF)
        for copy in copies_r2(h):
            copy.start()

    def hand_over(h):
        for copy in copies_r2(h):
            copy.wait_recv()
        for i in range(2):
            dq = dq_st[h, y, i].astype(F32) + r2_q[h, 0, i].astype(F32) + r2_q[h, 1, i].astype(F32)
            dkv = dkv_st[h, z, i].astype(F32) + r2_kv[h, 0, i].astype(F32) + r2_kv[h, 1, i].astype(F32)
            for k in range(2):
                g_q[h, 2 * i + k] = dq[:, k * TOK : (k + 1) * TOK].astype(BF)
                g_kv[h, 2 * i + k] = dkv[k * TOK : (k + 1) * TOK, :].astype(BF)
        for r in others:
            for copy in copies_g(h, r):
                copy.start()
        f_q[HG * x + h] = g_q[h, x]
        f_kv[HG * x + h] = g_kv[h, x]

    start_a(0)
    spread(0)
    start_a(1)
    forward(0)

    def step(h, carry):
        @pl.when(h < HG)
        def _():
            receive(h)

        @pl.when(h < HG - 2)
        def _():
            start_a(h + 2)

        @pl.when(h < HG)
        def _():
            phase1(h, 0)

        @pl.when(h < HG - 1)
        def _():
            spread(h + 1)

        @pl.when((h > 1) & (h < HG))
        def _():
            hand_over(h - 2)

        @pl.when(h > 0)
        def _():
            phase2(h - 1, 1)

        @pl.when(h < HG)
        def _():
            phase1(h, 1)

        @pl.when(h < HG - 1)
        def _():
            forward(h + 1)

        @pl.when(h == HG)
        def _():
            hand_over(HG - 2)

        @pl.when(h > 0)
        def _():
            combine(h - 1)

        @pl.when(h < HG)
        def _():
            phase2(h, 0)

        @pl.when(h == HG)
        def _():
            hand_over(HG - 1)

        return carry

    lax.fori_loop(0, HG + 1, step, 0)

    def finish(h, carry):
        for r in others:
            for copy in arrive_g(h, r):
                copy.wait_recv()
            for copy in copies_a(h, r) + copies_g(h, r) + copies_b(h, r) + copies_f(h, r):
                copy.wait_send()
            copy_st(2 * h, r).wait_send()
            copy_st(2 * h + 1, r).wait_send()
        for copy in copies_b(h, 0) + copies_f(h, 0) + copies_r1(h) + copies_r2(h):
            copy.wait_send()
        return carry

    lax.fori_loop(0, HG, finish, 0)

    image_rows = image_grad.shape[0]
    for pair in range((heads + 1) // 2):
        both = 2 * pair + 1 < heads
        width = TOK if both else HEAD_DIM
        cols = slice(pair * TOK, pair * TOK + width)
        first, second = f_kv[2 * pair].astype(F32), f_kv[2 * pair + 1].astype(F32)
        query = jnp.concatenate([f_q[2 * pair], f_q[2 * pair + 1]], 0).astype(F32).T
        key = jnp.concatenate([first[:, :HEAD_DIM], second[:, :HEAD_DIM]], 1)
        value = jnp.concatenate([first[:, HEAD_DIM:], second[:, HEAD_DIM:]], 1)
        for i, whole in enumerate((query, key, value)):
            image_out[i, :, cols] = whole[:image_rows, :width].astype(BF)
            text_out[i, :, cols] = whole[image_rows:, :width].astype(BF)


def body(image_qkv, text_qkv, image_grad, text_grad, text_len):
    slots = SIDE * HG
    vmem = pl.BlockSpec(memory_space=pltpu.VMEM)
    return pl.pallas_call(
        kernel,
        out_shape=(
            jax.ShapeDtypeStruct(image_qkv.shape, BF),
            jax.ShapeDtypeStruct(text_qkv.shape, BF),
        ),
        in_specs=[pl.BlockSpec(memory_space=pltpu.SMEM), vmem, vmem, vmem, vmem],
        out_specs=(vmem, vmem),
        scratch_shapes=[
            pltpu.VMEM((slots, TOK, TOK), BF),
            pltpu.VMEM((slots, TOK, TOK), BF),
            pltpu.VMEM((HG, SIDE, SIDE, TOK, TOK), BF),
            pltpu.VMEM((HG, SIDE, SIDE, TOK, TOK), BF),
            pltpu.VMEM((HG, SIDE, HEAD_DIM, ROWS), BF),
            pltpu.VMEM((KEYS, 2 * ROWS), F32),
            pltpu.VMEM((2, KEYS, 2 * ROWS), BF),
            pltpu.VMEM((2, KEYS, 2 * ROWS), F32),
            pltpu.VMEM((KEYS, TOK), F32),
            pltpu.VMEM((2 * HG, SIDE, 6 * SIDE, TOK), F32),
            pltpu.VMEM((HG, SIDE, 2, HEAD_DIM, ROWS // 2), BF),
            pltpu.VMEM((HG, SIDE, 2, ROWS // 2, TOK), BF),
            pltpu.VMEM((HG, 2, HEAD_DIM, ROWS // 2), BF),
            pltpu.VMEM((HG, 2, ROWS // 2, TOK), BF),
            pltpu.VMEM((HG, 2, 2, HEAD_DIM, ROWS // 2), BF),
            pltpu.VMEM((HG, 2, 2, ROWS // 2, TOK), BF),
            pltpu.VMEM((HG, SIDE, HEAD_DIM, TOK), BF),
            pltpu.VMEM((HG, SIDE, TOK, TOK), BF),
            pltpu.VMEM((slots, HEAD_DIM, TOK), BF),
            pltpu.VMEM((slots, TOK, TOK), BF),
        ]
        + [
            pltpu.SemaphoreType.DMA(shape)
            for shape in [(2, HG, SIDE)] * 2
            + [(2, HG, SIDE * SIDE)] * 2
            + [(2 * HG, SIDE)] * 2
            + [(2, HG, SIDE)] * 4
        ],
        compiler_params=pltpu.CompilerParams(
            collective_id=0, has_side_effects=True, vmem_limit_bytes=60 * 2**20
        ),
    )(text_len, image_qkv, text_qkv, image_grad, text_grad)


def solution(mesh):
    return jax.shard_map(
        body,
        mesh=mesh,
        in_specs=(
            P(None, "seq", "head"),
            P(None, "seq", "head"),
            P("seq", "head"),
            P("seq", "head"),
            P(),
        ),
        out_specs=(P(None, "seq", "head"), P(None, "seq", "head")),
        check_vma=False,
    )
```

```python
import jax
import jax.numpy as jnp
from jax import lax
from jax.experimental import pallas as pl
from jax.experimental.pallas import tpu as pltpu
from jax.sharding import PartitionSpec as P

F32 = jnp.float32
BF = jnp.bfloat16
MESH = pl.DeviceIdType.MESH
NT = (((1,), (1,)), ((), ()))
NN = (((1,), (0,)), ((), ()))
HEAD_DIM = 64
SIDE = 4
HG = 5
TOK = 128
ROWS = SIDE * TOK
KEYS = SIDE * ROWS
SCALE = HEAD_DIM**-0.5
LOG = SCALE * 1.4426950408889634
NEG = -1e30
CHUNK = 256


def dot(a, b, dims):
    return lax.dot_general(a, b, dims, preferred_element_type=F32)


def kernel(
    tl_ref, image_qkv, text_qkv, image_grad, text_grad, image_out, text_out,
    qg_own, kv_own, qg_all, kv_all, kt_all, s_ref, p_ref, dp_ref, acc, st,
    dq_st, dkv_st, r1_q, r1_kv, r2_q, r2_kv, g_q, g_kv, f_q, f_kv,
    sent, a_r, b_r, f_r, st_r, r_r, g_r,
):
    seq = lax.axis_index("seq")
    core = lax.axis_index("head")
    y, z, x = seq // 16, lax.rem(seq // 4, 4), lax.rem(seq, 4)

    def fwd(i, r):
        return lax.rem(i + r, SIDE)

    def back(i, r):
        return lax.rem(i + SIDE - r, SIDE)

    def at_x(i):
        return (y * 16 + z * 4 + i, core)

    def at_y(i):
        return (i * 16 + z * 4 + x, core)

    def at_z(i):
        return (y * 16 + i * 4 + x, core)

    def remote(src, dst, send, recv, device):
        return pltpu.make_async_remote_copy(
            src_ref=src, dst_ref=dst, send_sem=send, recv_sem=recv,
            device_id=device, device_id_type=MESH,
        )

    others = range(1, SIDE)

    def copies_a(h, r):
        t = fwd(x, r)
        return [
            remote(qg_own.at[HG * t + h], qg_all.at[h, y, x], sent.at[0], a_r.at[h, r - 1], at_x(t)),
            remote(kv_own.at[HG * t + h], kv_all.at[h, z, x], sent.at[0], a_r.at[h, r - 1], at_x(t)),
        ]

    def arrived(ref, sem):
        remote(ref, ref, sem, sem, (seq, core)).wait_recv()

    def gone(ref, sem):
        remote(ref, ref, sem, sem, (seq, core)).wait_send()

    def copies_b(h, r):
        f = back(x, r)
        q, k = qg_all.at[h, y, f], kv_all.at[h, z, f]
        sems = (sent.at[1], b_r.at[h, r])
        return [
            remote(q, q, *sems, at_y(fwd(y, 1))),
            remote(k, k, *sems, at_z(fwd(z, 1))),
            remote(q, q, *sems, at_y(back(y, 1))),
            remote(k, k, *sems, at_z(back(z, 1))),
        ]

    def copies_f(h, r):
        come, go = (back, fwd) if r % 2 == 0 else (fwd, back)
        f = back(x, r)
        q, k = qg_all.at[h, come(y, 1), f], kv_all.at[h, come(z, 1), f]
        sems = (sent.at[2], f_r.at[h])
        return [remote(q, q, *sems, at_y(go(y, 1))), remote(k, k, *sems, at_z(go(z, 1)))]

    def copy_st(u, r):
        return remote(st.at[u, 0], st.at[u, r], sent.at[3], st_r.at[u], at_y(fwd(y, r)))

    def copies_r1(h):
        yo, zo = fwd(y, 2), fwd(z, 2)
        places = ((at_y(fwd(y, 1)), at_z(fwd(z, 1))), (at_y(back(y, 1)), at_z(back(z, 1))))
        copies = []
        for n, (to_y, to_z) in enumerate(places):
            copies.append(remote(dq_st.at[h, yo, n], r1_q.at[h, n], sent.at[4], r_r.at[0, h], to_y))
            copies.append(remote(dkv_st.at[h, zo, n], r1_kv.at[h, n], sent.at[5], r_r.at[1, h], to_z))
        return copies

    def copies_r2(h):
        copies = []
        for n, (ty, tz) in enumerate(((fwd(y, 1), fwd(z, 1)), (back(y, 1), back(z, 1)))):
            k = 2 + n
            copies.append(remote(dq_st.at[h, ty], r2_q.at[h, n], sent.at[6], r_r.at[2, h], at_y(ty)))
            copies.append(remote(dkv_st.at[h, tz], r2_kv.at[h, n], sent.at[7], r_r.at[3, h], at_z(tz)))
        return copies

    def copies_g(h, r):
        t = fwd(x, r)
        return [
            remote(g_q.at[h, t], f_q.at[HG * x + h], sent.at[8], g_r.at[0, h], at_x(t)),
            remote(g_kv.at[h, t], f_kv.at[HG * x + h], sent.at[9], g_r.at[1, h], at_x(t)),
        ]

    barrier = pltpu.get_barrier_semaphore()
    for r in others:
        for place in (at_x(fwd(x, r)), at_y(fwd(y, r)), at_z(fwd(z, r))):
            pl.semaphore_signal(barrier, inc=1, device_id=place, device_id_type=MESH)

    def column(image, text, pair):
        cols = slice(pair * TOK, min((pair + 1) * TOK, image.shape[-1]))
        return jnp.concatenate([image[:, cols].astype(F32), text[:, cols].astype(F32)], 0)

    heads = image_grad.shape[1] // HEAD_DIM
    for pair in range((heads + 1) // 2):
        query, key, value = (column(image_qkv.at[i], text_qkv.at[i], pair) for i in range(3))
        grad = column(image_grad, text_grad, pair)
        for own, left, right in ((qg_own, query, grad), (kv_own, key, value)):
            own[2 * pair] = jnp.concatenate([left[:, :HEAD_DIM], right[:, :HEAD_DIM]], 1).astype(BF)
            if 2 * pair + 1 < heads:
                own[2 * pair + 1] = jnp.concatenate([left[:, HEAD_DIM:], right[:, HEAD_DIM:]], 1).astype(BF)
    for slot in range(heads, SIDE * HG):
        qg_own[slot] = jnp.zeros((TOK, TOK), BF)
        kv_own[slot] = jnp.zeros((TOK, TOK), BF)

    pl.semaphore_wait(barrier, 3 * (SIDE - 1))

    def start_a(h):
        for r in others:
            for copy in copies_a(h, r):
                copy.start()
        qg_all[h, y, x] = qg_own[HG * x + h]
        kv_all[h, z, x] = kv_own[HG * x + h]

    order = (0, 1, 3, 2)

    def spread(h):
        for r in order:
            if r:
                arrived(qg_all.at[h, 0, pl.ds(0, 2)], a_r.at[h, r - 1])
            for copy in copies_b(h, r):
                copy.start()

    def forward(h):
        for r in order:
            arrived(qg_all.at[h, 0], b_r.at[h, r])
            for copy in copies_f(h, r):
                copy.start()

    def receive(h):
        arrived(qg_all.at[h, pl.ds(0, 2)], f_r.at[h])
        for k in range(SIDE):
            kt_all[h, k] = kv_all[h, k].reshape(ROWS, TOK).T[:HEAD_DIM]

    def phase1(h, half):
        count = 2 * ROWS
        qg = qg_all[h, 2 * half : 2 * half + 2].reshape(count, TOK)
        lane = lax.broadcasted_iota(jnp.int32, qg.shape, 1)
        q0 = jnp.where(lane < HEAD_DIM, qg, jnp.zeros_like(qg))
        g0 = jnp.where(lane < HEAD_DIM, jnp.zeros_like(qg), qg)
        sub = lax.broadcasted_iota(jnp.int32, (8, count), 0)
        top = jnp.full((8, count), NEG, F32)
        for k in range(SIDE):
            s = dot(kv_all[h, k].reshape(ROWS, TOK), q0, NT)
            s_ref[k * ROWS : (k + 1) * ROWS, :] = s
            parts = s.reshape(SIDE, TOK // 8, 8, count)
            top = jnp.maximum(top, jnp.max(parts[:, : TOK // 8 - 1].reshape(-1, 8, count), axis=0))
            for i in range(SIDE):
                valid = (y * 16 + k * 4 + i) * 8 + sub < tl_ref[0]
                text = jnp.where(valid, parts[i, TOK // 8 - 1], NEG)
                end = k * ROWS + (i + 1) * TOK
                s_ref[end - 8 : end, :] = text
                top = jnp.maximum(top, text)
        top = jnp.max(top, axis=0, keepdims=True) * LOG
        total = jnp.zeros((8, count), F32)
        weighted = jnp.zeros((8, count), F32)
        for k in range(SIDE):
            rows = slice(k * ROWS, (k + 1) * ROWS)
            d = dot(kv_all[h, k].reshape(ROWS, TOK), g0, NT)
            p = jnp.exp2(s_ref[rows, :] * LOG - top)
            total += jnp.sum(p.reshape(-1, 8, count), axis=0)
            weighted += jnp.sum((p * d).reshape(-1, 8, count), axis=0)
            p_ref[half, rows, :] = p.astype(BF)
            dp_ref[half, rows, :] = d
        stats = (top, jnp.sum(total, axis=0, keepdims=True), jnp.sum(weighted, axis=0, keepdims=True))
        parts = [s[:, i * TOK : (i + 1) * TOK] for s in stats for i in range(2 * SIDE)]
        st[2 * h + half, 0] = jnp.concatenate(parts, 0)
        for r in others:
            copy_st(2 * h + half, r).start()

    def phase2(h, half):
        u = 2 * h + half
        arrived(st.at[u, pl.ds(1, SIDE - 1)], st_r.at[u])
        stats = [st[u, r] for r in range(SIDE)]
        tops = [s[0:8] for s in stats]
        top = jnp.maximum(jnp.maximum(tops[0], tops[1]), jnp.maximum(tops[2], tops[3]))
        parts = [jnp.exp2(t - top) for t in tops]
        total = sum(s[8:16] * e for s, e in zip(stats, parts))
        factors = parts[0] / total
        deltas = sum(s[16:24] * e for s, e in zip(stats, parts)) / total
        for j in range(2):
            factor, delta = (
                jnp.concatenate([v[i : i + 1] for i in range(SIDE * j, SIDE * (j + 1))], 1)
                for v in (factors, deltas)
            )
            qg = qg_all[h, 2 * half + j].reshape(ROWS, TOK)
            lane = lax.broadcasted_iota(jnp.int32, qg.shape, 1)
            q0 = jnp.where(lane < HEAD_DIM, qg, jnp.zeros_like(qg))
            g0 = jnp.where(lane < HEAD_DIM, jnp.zeros_like(qg), qg)
            cols = slice(j * ROWS, (j + 1) * ROWS)
            dq = jnp.zeros((HEAD_DIM, ROWS), F32)
            for c in range(KEYS // CHUNK):
                rows = slice(c * CHUNK, (c + 1) * CHUNK)
                p = p_ref[half, rows, cols].astype(F32) * factor
                ds = (p * (dp_ref[half, rows, cols] - delta)).astype(BF)
                part = dot(p.astype(BF), g0, NN) + dot(ds, q0, NN)
                if half == 0 and j == 0:
                    acc[rows, :] = part
                else:
                    acc[rows, :] += part
                per = ROWS // CHUNK
                at = c % per * CHUNK
                dq += dot(kt_all[h, c // per, :, at : at + CHUNK], ds, NN)
            dq = (dq * SCALE).astype(BF)
            for i in range(2):
                dq_st[h, 2 * half + j, i] = dq[:, i * ROWS // 2 : (i + 1) * ROWS // 2]
        if half == 1:
            lane = lax.broadcasted_iota(jnp.int32, (ROWS, TOK), 1)
            for k in range(SIDE):
                rows = slice(k * ROWS, (k + 1) * ROWS)
                dkv = (acc[rows, :] * jnp.where(lane < HEAD_DIM, SCALE, 1.0)).astype(BF)
                dkv_st[h, k] = dkv.reshape(2, ROWS // 2, TOK)
            for copy in copies_r1(h):
                copy.start()

    def combine(h):
        arrived(r1_q.at[h], r_r.at[0, h])
        arrived(r1_kv.at[h], r_r.at[1, h])
        for n, (ty, tz) in enumerate(((fwd(y, 1), fwd(z, 1)), (back(y, 1), back(z, 1)))):
            dq_st[h, ty, n] = (dq_st[h, ty, n].astype(F32) + r1_q[h, n].astype(F32)).astype(BF)
            dkv_st[h, tz, n] = (dkv_st[h, tz, n].astype(F32) + r1_kv[h, n].astype(F32)).astype(BF)
        for copy in copies_r2(h):
            copy.start()

    def hand_over(h):
        arrived(r2_q.at[h], r_r.at[2, h])
        arrived(r2_kv.at[h], r_r.at[3, h])
        for i in range(2):
            dq = dq_st[h, y, i].astype(F32) + r2_q[h, 0, i].astype(F32) + r2_q[h, 1, i].astype(F32)
            dkv = dkv_st[h, z, i].astype(F32) + r2_kv[h, 0, i].astype(F32) + r2_kv[h, 1, i].astype(F32)
            for k in range(2):
                g_q[h, 2 * i + k] = dq[:, k * TOK : (k + 1) * TOK].astype(BF)
                g_kv[h, 2 * i + k] = dkv[k * TOK : (k + 1) * TOK, :].astype(BF)
        for r in others:
            for copy in copies_g(h, r):
                copy.start()
        f_q[HG * x + h] = g_q[h, x]
        f_kv[HG * x + h] = g_kv[h, x]

    start_a(0)
    spread(0)
    start_a(1)
    forward(0)

    def step(h, carry):
        @pl.when(h < HG)
        def _():
            receive(h)

        @pl.when(h < HG - 2)
        def _():
            start_a(h + 2)

        @pl.when(h < HG)
        def _():
            phase1(h, 0)

        @pl.when(h < HG - 1)
        def _():
            spread(h + 1)

        @pl.when((h > 1) & (h < HG))
        def _():
            hand_over(h - 2)

        @pl.when(h > 0)
        def _():
            phase2(h - 1, 1)

        @pl.when(h < HG)
        def _():
            phase1(h, 1)

        @pl.when(h < HG - 1)
        def _():
            forward(h + 1)

        @pl.when(h == HG)
        def _():
            hand_over(HG - 2)

        @pl.when(h > 0)
        def _():
            combine(h - 1)

        @pl.when(h < HG)
        def _():
            phase2(h, 0)

        @pl.when(h == HG)
        def _():
            hand_over(HG - 1)

        return carry

    lax.fori_loop(0, HG + 1, step, 0)

    def finish(h, carry):
        arrived(g_q.at[h, pl.ds(0, SIDE - 1)], g_r.at[0, h])
        arrived(g_kv.at[h, pl.ds(0, SIDE - 1)], g_r.at[1, h])
        return carry

    lax.fori_loop(0, HG, finish, 0)
    moved = (
        qg_all.at[:, pl.ds(0, 2), pl.ds(0, SIDE - 1)],
        qg_all,
        qg_all.at[:, pl.ds(0, 2)],
        st.at[:, pl.ds(0, SIDE - 1)],
        r1_q,
        r1_kv,
        r2_q,
        r2_kv,
        g_q.at[:, pl.ds(0, SIDE - 1)],
        g_kv.at[:, pl.ds(0, SIDE - 1)],
    )
    for i, ref in enumerate(moved):
        gone(ref, sent.at[i])

    image_rows = image_grad.shape[0]
    for pair in range((heads + 1) // 2):
        both = 2 * pair + 1 < heads
        width = TOK if both else HEAD_DIM
        cols = slice(pair * TOK, pair * TOK + width)
        first, second = f_kv[2 * pair].astype(F32), f_kv[2 * pair + 1].astype(F32)
        query = jnp.concatenate([f_q[2 * pair], f_q[2 * pair + 1]], 0).astype(F32).T
        key = jnp.concatenate([first[:, :HEAD_DIM], second[:, :HEAD_DIM]], 1)
        value = jnp.concatenate([first[:, HEAD_DIM:], second[:, HEAD_DIM:]], 1)
        for i, whole in enumerate((query, key, value)):
            image_out[i, :, cols] = whole[:image_rows, :width].astype(BF)
            text_out[i, :, cols] = whole[image_rows:, :width].astype(BF)


def body(image_qkv, text_qkv, image_grad, text_grad, text_len):
    slots = SIDE * HG
    vmem = pl.BlockSpec(memory_space=pltpu.VMEM)
    return pl.pallas_call(
        kernel,
        out_shape=(
            jax.ShapeDtypeStruct(image_qkv.shape, BF),
            jax.ShapeDtypeStruct(text_qkv.shape, BF),
        ),
        in_specs=[pl.BlockSpec(memory_space=pltpu.SMEM), vmem, vmem, vmem, vmem],
        out_specs=(vmem, vmem),
        scratch_shapes=[
            pltpu.VMEM((slots, TOK, TOK), BF),
            pltpu.VMEM((slots, TOK, TOK), BF),
            pltpu.VMEM((HG, SIDE, SIDE, TOK, TOK), BF),
            pltpu.VMEM((HG, SIDE, SIDE, TOK, TOK), BF),
            pltpu.VMEM((HG, SIDE, HEAD_DIM, ROWS), BF),
            pltpu.VMEM((KEYS, 2 * ROWS), F32),
            pltpu.VMEM((2, KEYS, 2 * ROWS), BF),
            pltpu.VMEM((2, KEYS, 2 * ROWS), F32),
            pltpu.VMEM((KEYS, TOK), F32),
            pltpu.VMEM((2 * HG, SIDE, 6 * SIDE, TOK), F32),
            pltpu.VMEM((HG, SIDE, 2, HEAD_DIM, ROWS // 2), BF),
            pltpu.VMEM((HG, SIDE, 2, ROWS // 2, TOK), BF),
            pltpu.VMEM((HG, 2, HEAD_DIM, ROWS // 2), BF),
            pltpu.VMEM((HG, 2, ROWS // 2, TOK), BF),
            pltpu.VMEM((HG, 2, 2, HEAD_DIM, ROWS // 2), BF),
            pltpu.VMEM((HG, 2, 2, ROWS // 2, TOK), BF),
            pltpu.VMEM((HG, SIDE, HEAD_DIM, TOK), BF),
            pltpu.VMEM((HG, SIDE, TOK, TOK), BF),
            pltpu.VMEM((slots, HEAD_DIM, TOK), BF),
            pltpu.VMEM((slots, TOK, TOK), BF),
        ]
        + [
            pltpu.SemaphoreType.DMA(shape)
            for shape in [(10,), (HG, SIDE - 1), (HG, SIDE), (HG,), (2 * HG,), (4, HG), (2, HG)]
        ],
        compiler_params=pltpu.CompilerParams(
            collective_id=0, has_side_effects=True, vmem_limit_bytes=60 * 2**20
        ),
    )(text_len, image_qkv, text_qkv, image_grad, text_grad)


def solution(mesh):
    return jax.shard_map(
        body,
        mesh=mesh,
        in_specs=(
            P(None, "seq", "head"),
            P(None, "seq", "head"),
            P("seq", "head"),
            P("seq", "head"),
            P(),
        ),
        out_specs=(P(None, "seq", "head"), P(None, "seq", "head")),
        check_vma=False,
    )
```

```python
import jax
import jax.numpy as jnp
from jax import lax
from jax.experimental import pallas as pl
from jax.experimental.pallas import tpu as pltpu
from jax.sharding import PartitionSpec as P

F32 = jnp.float32
BF = jnp.bfloat16
MESH = pl.DeviceIdType.MESH
NT = (((1,), (1,)), ((), ()))
NN = (((1,), (0,)), ((), ()))
HEAD_DIM = 64
SIDE = 4
HG = 5
TOK = 128
ROWS = SIDE * TOK
KEYS = SIDE * ROWS
SCALE = HEAD_DIM**-0.5
LOG = SCALE * 1.4426950408889634
NEG = -1e30
CHUNK = 256


def dot(a, b, dims):
    return lax.dot_general(a, b, dims, preferred_element_type=F32)


def kernel(
    tl_ref, image_qkv, text_qkv, image_grad, text_grad, image_out, text_out,
    qg_own, kv_own, qg_all, kv_all, kt_all, s_ref, p_ref, dp_ref, acc, st,
    dq_st, dkv_st, r1_q, r1_kv, r2_q, r2_kv, g_q, g_kv, f_q, f_kv,
    sent, a_r, b_r, f_r, st_r, r_r, g_r,
):
    seq = lax.axis_index("seq")
    core = lax.axis_index("head")
    y, z, x = seq // 16, lax.rem(seq // 4, 4), lax.rem(seq, 4)

    def fwd(i, r):
        return lax.rem(i + r, SIDE)

    def back(i, r):
        return lax.rem(i + SIDE - r, SIDE)

    def at_x(i):
        return (y * 16 + z * 4 + i, core)

    def at_y(i):
        return (i * 16 + z * 4 + x, core)

    def at_z(i):
        return (y * 16 + i * 4 + x, core)

    def remote(src, dst, send, recv, device):
        return pltpu.make_async_remote_copy(
            src_ref=src, dst_ref=dst, send_sem=send, recv_sem=recv,
            device_id=device, device_id_type=MESH,
        )

    others = range(1, SIDE)

    def copies_a(h, r):
        t = fwd(x, r)
        return [
            remote(qg_own.at[HG * t + h], qg_all.at[h, y, x], sent.at[0], a_r.at[h, r - 1], at_x(t)),
            remote(kv_own.at[HG * t + h], kv_all.at[h, z, x], sent.at[0], a_r.at[h, r - 1], at_x(t)),
        ]

    def arrived(ref, sem):
        remote(ref, ref, sem, sem, (seq, core)).wait_recv()

    def gone(ref, sem):
        remote(ref, ref, sem, sem, (seq, core)).wait_send()

    def copies_b(h, r):
        f = back(x, r)
        q, k = qg_all.at[h, y, f], kv_all.at[h, z, f]
        sems = (sent.at[1], b_r.at[h, r])
        return [
            remote(q, q, *sems, at_y(fwd(y, 1))),
            remote(k, k, *sems, at_z(fwd(z, 1))),
            remote(q, q, *sems, at_y(back(y, 1))),
            remote(k, k, *sems, at_z(back(z, 1))),
        ]

    def copies_f(h, r):
        come, go = (back, fwd) if r % 2 == 0 else (fwd, back)
        f = back(x, r)
        q, k = qg_all.at[h, come(y, 1), f], kv_all.at[h, come(z, 1), f]
        sems = (sent.at[2], f_r.at[h])
        return [remote(q, q, *sems, at_y(go(y, 1))), remote(k, k, *sems, at_z(go(z, 1)))]

    def copy_st(u, r):
        return remote(st.at[u, 0], st.at[u, r], sent.at[3], st_r.at[u], at_y(fwd(y, r)))

    def copies_r1(h, kv):
        src, dst, at, i = (dkv_st, r1_kv, at_z, z) if kv else (dq_st, r1_q, at_y, y)
        return [
            remote(src.at[h, fwd(i, 2), n], dst.at[h, n], sent.at[4 + kv], r_r.at[kv, h], at(t))
            for n, t in enumerate((fwd(i, 1), back(i, 1)))
        ]

    def copies_r2(h, kv):
        if not kv:
            return [
                remote(dq_st.at[h, t], r2_q.at[h, n], sent.at[6], r_r.at[2, h], at_y(t))
                for n, t in enumerate((fwd(y, 1), back(y, 1)))
            ]
        return [
            remote(dkv_st.at[h, t, i], r2_kv.at[h, n, i], sent.at[7], r_r.at[3 + i, h], at_z(t))
            for i in range(2)
            for n, t in enumerate((fwd(z, 1), back(z, 1)))
        ]

    def copy_g(h, r, kv):
        src, dst = (g_kv, f_kv) if kv else (g_q, f_q)
        t = fwd(x, r)
        return remote(src.at[h, t], dst.at[HG * x + h], sent.at[8 + kv], g_r.at[kv, h], at_x(t))

    barrier = pltpu.get_barrier_semaphore()
    for r in others:
        for place in (at_x(fwd(x, r)), at_y(fwd(y, r)), at_z(fwd(z, r))):
            pl.semaphore_signal(barrier, inc=1, device_id=place, device_id_type=MESH)

    def column(image, text, pair):
        cols = slice(pair * TOK, min((pair + 1) * TOK, image.shape[-1]))
        return jnp.concatenate([image[:, cols].astype(F32), text[:, cols].astype(F32)], 0)

    heads = image_grad.shape[1] // HEAD_DIM
    for pair in range((heads + 1) // 2):
        query, key, value = (column(image_qkv.at[i], text_qkv.at[i], pair) for i in range(3))
        grad = column(image_grad, text_grad, pair)
        for own, left, right in ((qg_own, query, grad), (kv_own, key, value)):
            own[2 * pair] = jnp.concatenate([left[:, :HEAD_DIM], right[:, :HEAD_DIM]], 1).astype(BF)
            if 2 * pair + 1 < heads:
                own[2 * pair + 1] = jnp.concatenate([left[:, HEAD_DIM:], right[:, HEAD_DIM:]], 1).astype(BF)
    for slot in range(heads, SIDE * HG):
        qg_own[slot] = jnp.zeros((TOK, TOK), BF)
        kv_own[slot] = jnp.zeros((TOK, TOK), BF)

    pl.semaphore_wait(barrier, 3 * (SIDE - 1))

    def start_a(h):
        for r in others:
            for copy in copies_a(h, r):
                copy.start()
        qg_all[h, y, x] = qg_own[HG * x + h]
        kv_all[h, z, x] = kv_own[HG * x + h]

    order = (0, 1, 3, 2)

    def spread(h):
        for r in order:
            if r:
                arrived(qg_all.at[h, 0, pl.ds(0, 2)], a_r.at[h, r - 1])
            for copy in copies_b(h, r):
                copy.start()

    def forward(h):
        for r in order:
            arrived(qg_all.at[h, 0], b_r.at[h, r])
            for copy in copies_f(h, r):
                copy.start()

    def receive(h):
        arrived(qg_all.at[h, pl.ds(0, 2)], f_r.at[h])
        for k in range(SIDE):
            kt_all[h, k] = kv_all[h, k].reshape(ROWS, TOK).T[:HEAD_DIM]

    def phase1(h, half):
        count = 2 * ROWS
        qg = qg_all[h, 2 * half : 2 * half + 2].reshape(count, TOK)
        lane = lax.broadcasted_iota(jnp.int32, qg.shape, 1)
        q0 = jnp.where(lane < HEAD_DIM, qg, jnp.zeros_like(qg))
        g0 = jnp.where(lane < HEAD_DIM, jnp.zeros_like(qg), qg)
        sub = lax.broadcasted_iota(jnp.int32, (8, count), 0)
        top = jnp.full((8, count), NEG, F32)
        for k in range(SIDE):
            s = dot(kv_all[h, k].reshape(ROWS, TOK), q0, NT)
            s_ref[k * ROWS : (k + 1) * ROWS, :] = s
            parts = s.reshape(SIDE, TOK // 8, 8, count)
            top = jnp.maximum(top, jnp.max(parts[:, : TOK // 8 - 1].reshape(-1, 8, count), axis=0))
            for i in range(SIDE):
                valid = (y * 16 + k * 4 + i) * 8 + sub < tl_ref[0]
                text = jnp.where(valid, parts[i, TOK // 8 - 1], NEG)
                end = k * ROWS + (i + 1) * TOK
                s_ref[end - 8 : end, :] = text
                top = jnp.maximum(top, text)
        top = jnp.max(top, axis=0, keepdims=True) * LOG
        total = jnp.zeros((8, count), F32)
        weighted = jnp.zeros((8, count), F32)
        for k in range(SIDE):
            rows = slice(k * ROWS, (k + 1) * ROWS)
            d = dot(kv_all[h, k].reshape(ROWS, TOK), g0, NT)
            p = jnp.exp2(s_ref[rows, :] * LOG - top)
            total += jnp.sum(p.reshape(-1, 8, count), axis=0)
            weighted += jnp.sum((p * d).reshape(-1, 8, count), axis=0)
            p_ref[half, rows, :] = p.astype(BF)
            dp_ref[half, rows, :] = d
        stats = (top, jnp.sum(total, axis=0, keepdims=True), jnp.sum(weighted, axis=0, keepdims=True))
        parts = [s[:, i * TOK : (i + 1) * TOK] for s in stats for i in range(2 * SIDE)]
        st[2 * h + half, 0] = jnp.concatenate(parts, 0)
        for r in others:
            copy_st(2 * h + half, r).start()

    def row_terms(u):
        arrived(st.at[u, pl.ds(1, SIDE - 1)], st_r.at[u])
        stats = [st[u, r] for r in range(SIDE)]
        tops = [s[0:8] for s in stats]
        top = jnp.maximum(jnp.maximum(tops[0], tops[1]), jnp.maximum(tops[2], tops[3]))
        parts = [jnp.exp2(t - top) for t in tops]
        total = sum(s[8:16] * e for s, e in zip(stats, parts))
        factors = parts[0] / total
        deltas = sum(s[16:24] * e for s, e in zip(stats, parts)) / total
        return [
            [jnp.concatenate([v[i : i + 1] for i in range(SIDE * j, SIDE * (j + 1))], 1) for v in (factors, deltas)]
            for j in range(2)
        ]

    def apart(qg):
        lane = lax.broadcasted_iota(jnp.int32, qg.shape, 1)
        zero = jnp.zeros_like(qg)
        return jnp.where(lane < HEAD_DIM, qg, zero), jnp.where(lane < HEAD_DIM, zero, qg)

    def keep_dq(h, slot, dq):
        dq = (dq * SCALE).astype(BF)
        for i in range(2):
            dq_st[h, slot, i] = dq[:, i * ROWS // 2 : (i + 1) * ROWS // 2]

    def keep_dkv(h, k, dkv):
        lane = lax.broadcasted_iota(jnp.int32, dkv.shape, 1)
        dkv = (dkv * jnp.where(lane < HEAD_DIM, SCALE, 1.0)).astype(BF)
        dkv_st[h, k] = dkv.reshape(2, ROWS // 2, TOK)

    def phase2(h, half):
        terms = row_terms(2 * h + half)
        for j in range(2):
            factor, delta = terms[j]
            q0, g0 = apart(qg_all[h, 2 * half + j].reshape(ROWS, TOK))
            cols = slice(j * ROWS, (j + 1) * ROWS)
            dq = jnp.zeros((HEAD_DIM, ROWS), F32)
            for c in range(KEYS // CHUNK):
                rows = slice(c * CHUNK, (c + 1) * CHUNK)
                p = p_ref[half, rows, cols].astype(F32) * factor
                ds = (p * (dp_ref[half, rows, cols] - delta)).astype(BF)
                part = dot(p.astype(BF), g0, NN) + dot(ds, q0, NN)
                if half == 0 and j == 0:
                    acc[rows, :] = part
                else:
                    acc[rows, :] += part
                per = ROWS // CHUNK
                at = c % per * CHUNK
                dq += dot(kt_all[h, c // per, :, at : at + CHUNK], ds, NN)
            keep_dq(h, 2 * half + j, dq)
        if half == 1:
            for k in range(SIDE):
                keep_dkv(h, k, acc[k * ROWS : (k + 1) * ROWS, :])
            for copy in copies_r1(h, 0) + copies_r1(h, 1):
                copy.start()

    def combine_q(h):
        arrived(r1_q.at[h], r_r.at[0, h])
        for n, t in enumerate((fwd(y, 1), back(y, 1))):
            dq_st[h, t, n] = (dq_st[h, t, n].astype(F32) + r1_q[h, n].astype(F32)).astype(BF)
        for copy in copies_r2(h, 0):
            copy.start()

    def combine_kv(h):
        arrived(r1_kv.at[h], r_r.at[1, h])
        for n, t in enumerate((fwd(z, 1), back(z, 1))):
            dkv_st[h, t, n] = (dkv_st[h, t, n].astype(F32) + r1_kv[h, n].astype(F32)).astype(BF)
        for copy in copies_r2(h, 1):
            copy.start()

    def last_unit():
        h = HG - 1
        terms = row_terms(2 * h + 1)
        q0, g0 = apart(qg_all[h, 2:4].reshape(2 * ROWS, TOK))

        def scores(k, dqs):
            out = []
            for j, dq in enumerate(dqs):
                factor, delta = terms[j]
                cols = slice(j * ROWS, (j + 1) * ROWS)
                for c in range(ROWS // CHUNK):
                    rows = pl.ds(pl.multiple_of(k * ROWS + c * CHUNK, CHUNK), CHUNK)
                    p = p_ref[1, rows, cols].astype(F32) * factor
                    ds = (p * (dp_ref[1, rows, cols] - delta)).astype(BF)
                    p_ref[1, rows, cols] = p.astype(BF)
                    p_ref[0, rows, cols] = ds
                    dq += dot(kt_all[h, k, :, c * CHUNK : (c + 1) * CHUNK], ds, NN)
                out.append(dq)
            return out

        def sums(k):
            rows = pl.ds(pl.multiple_of(k * ROWS, ROWS), ROWS)
            keep_dkv(h, k, acc[rows, :] + dot(p_ref[1, rows, :], g0, NN) + dot(p_ref[0, rows, :], q0, NN))

        dqs = [jnp.zeros((HEAD_DIM, ROWS), F32)] * 2
        far, near, own = fwd(z, 2), (fwd(z, 1), back(z, 1)), z
        dqs = scores(far, dqs)
        sums(far)
        for copy in copies_r1(h, 1):
            copy.start()
        for k in near + (own,):
            dqs = scores(k, dqs)
        for j in range(2):
            keep_dq(h, 2 + j, dqs[j])
        for copy in copies_r1(h, 0):
            copy.start()
        for k in near:
            sums(k)
        hand_over(HG - 2)
        combine_kv(h)
        combine_q(h)
        sums(own)

    def hand_over(h):
        arrived(r2_q.at[h], r_r.at[2, h])
        for i in range(2):
            dq = dq_st[h, y, i].astype(F32) + r2_q[h, 0, i].astype(F32) + r2_q[h, 1, i].astype(F32)
            for k in range(2):
                g_q[h, 2 * i + k] = dq[:, k * TOK : (k + 1) * TOK].astype(BF)
        for r in (2, 1, 3):
            copy_g(h, r, 0).start()
        for i in range(2):
            arrived(r2_kv.at[h, 0], r_r.at[3 + i, h])
            dkv = dkv_st[h, z, i].astype(F32) + r2_kv[h, 0, i].astype(F32) + r2_kv[h, 1, i].astype(F32)
            for k in range(2):
                g_kv[h, 2 * i + k] = dkv[k * TOK : (k + 1) * TOK, :].astype(BF)
            for r in (2, 1, 3):

                @pl.when(fwd(x, r) // 2 == i)
                def _():
                    copy_g(h, r, 1).start()

        f_q[HG * x + h] = g_q[h, x]
        f_kv[HG * x + h] = g_kv[h, x]

    start_a(0)
    spread(0)
    start_a(1)
    forward(0)

    def step(h, carry):
        receive(h)

        @pl.when(h < HG - 2)
        def _():
            start_a(h + 2)

        phase1(h, 0)

        @pl.when(h < HG - 1)
        def _():
            spread(h + 1)

        @pl.when(h > 1)
        def _():
            hand_over(h - 2)

        @pl.when(h > 0)
        def _():
            phase2(h - 1, 1)

        phase1(h, 1)

        @pl.when(h < HG - 1)
        def _():
            forward(h + 1)

        @pl.when(h > 0)
        def _():
            combine_q(h - 1)
            combine_kv(h - 1)

        phase2(h, 0)
        return carry

    lax.fori_loop(0, HG, step, 0)
    last_unit()
    hand_over(HG - 1)

    def finish(h, carry):
        arrived(g_q.at[h, pl.ds(0, SIDE - 1)], g_r.at[0, h])
        arrived(g_kv.at[h, pl.ds(0, SIDE - 1)], g_r.at[1, h])
        return carry

    lax.fori_loop(0, HG, finish, 0)
    moved = (
        qg_all.at[:, pl.ds(0, 2), pl.ds(0, SIDE - 1)],
        qg_all,
        qg_all.at[:, pl.ds(0, 2)],
        st.at[:, pl.ds(0, SIDE - 1)],
        r1_q,
        r1_kv,
        r2_q,
        r2_kv,
        g_q.at[:, pl.ds(0, SIDE - 1)],
        g_kv.at[:, pl.ds(0, SIDE - 1)],
    )
    for i, ref in enumerate(moved):
        gone(ref, sent.at[i])

    image_rows = image_grad.shape[0]
    for pair in range((heads + 1) // 2):
        both = 2 * pair + 1 < heads
        width = TOK if both else HEAD_DIM
        cols = slice(pair * TOK, pair * TOK + width)
        first, second = f_kv[2 * pair].astype(F32), f_kv[2 * pair + 1].astype(F32)
        query = jnp.concatenate([f_q[2 * pair], f_q[2 * pair + 1]], 0).astype(F32).T
        key = jnp.concatenate([first[:, :HEAD_DIM], second[:, :HEAD_DIM]], 1)
        value = jnp.concatenate([first[:, HEAD_DIM:], second[:, HEAD_DIM:]], 1)
        for i, whole in enumerate((query, key, value)):
            image_out[i, :, cols] = whole[:image_rows, :width].astype(BF)
            text_out[i, :, cols] = whole[image_rows:, :width].astype(BF)


def body(image_qkv, text_qkv, image_grad, text_grad, text_len):
    slots = SIDE * HG
    vmem = pl.BlockSpec(memory_space=pltpu.VMEM)
    return pl.pallas_call(
        kernel,
        out_shape=(
            jax.ShapeDtypeStruct(image_qkv.shape, BF),
            jax.ShapeDtypeStruct(text_qkv.shape, BF),
        ),
        in_specs=[pl.BlockSpec(memory_space=pltpu.SMEM), vmem, vmem, vmem, vmem],
        out_specs=(vmem, vmem),
        scratch_shapes=[
            pltpu.VMEM((slots, TOK, TOK), BF),
            pltpu.VMEM((slots, TOK, TOK), BF),
            pltpu.VMEM((HG, SIDE, SIDE, TOK, TOK), BF),
            pltpu.VMEM((HG, SIDE, SIDE, TOK, TOK), BF),
            pltpu.VMEM((HG, SIDE, HEAD_DIM, ROWS), BF),
            pltpu.VMEM((KEYS, 2 * ROWS), F32),
            pltpu.VMEM((2, KEYS, 2 * ROWS), BF),
            pltpu.VMEM((2, KEYS, 2 * ROWS), F32),
            pltpu.VMEM((KEYS, TOK), F32),
            pltpu.VMEM((2 * HG, SIDE, 6 * SIDE, TOK), F32),
            pltpu.VMEM((HG, SIDE, 2, HEAD_DIM, ROWS // 2), BF),
            pltpu.VMEM((HG, SIDE, 2, ROWS // 2, TOK), BF),
            pltpu.VMEM((HG, 2, HEAD_DIM, ROWS // 2), BF),
            pltpu.VMEM((HG, 2, ROWS // 2, TOK), BF),
            pltpu.VMEM((HG, 2, 2, HEAD_DIM, ROWS // 2), BF),
            pltpu.VMEM((HG, 2, 2, ROWS // 2, TOK), BF),
            pltpu.VMEM((HG, SIDE, HEAD_DIM, TOK), BF),
            pltpu.VMEM((HG, SIDE, TOK, TOK), BF),
            pltpu.VMEM((slots, HEAD_DIM, TOK), BF),
            pltpu.VMEM((slots, TOK, TOK), BF),
        ]
        + [
            pltpu.SemaphoreType.DMA(shape)
            for shape in [(10,), (HG, SIDE - 1), (HG, SIDE), (HG,), (2 * HG,), (5, HG), (2, HG)]
        ],
        compiler_params=pltpu.CompilerParams(
            collective_id=0, has_side_effects=True, vmem_limit_bytes=60 * 2**20
        ),
    )(text_len, image_qkv, text_qkv, image_grad, text_grad)


def solution(mesh):
    return jax.shard_map(
        body,
        mesh=mesh,
        in_specs=(
            P(None, "seq", "head"),
            P(None, "seq", "head"),
            P("seq", "head"),
            P("seq", "head"),
            P(),
        ),
        out_specs=(P(None, "seq", "head"), P(None, "seq", "head")),
        check_vma=False,
    )
```

```python
import jax
import jax.numpy as jnp
from jax import lax
from jax.experimental import pallas as pl
from jax.experimental.pallas import tpu as pltpu
from jax.sharding import PartitionSpec as P

F32 = jnp.float32
BF = jnp.bfloat16
MESH = pl.DeviceIdType.MESH
NT = (((1,), (1,)), ((), ()))
NN = (((1,), (0,)), ((), ()))
HEAD_DIM = 64
SIDE = 4
HG = 5
TOK = 128
ROWS = SIDE * TOK
KEYS = SIDE * ROWS
SCALE = HEAD_DIM**-0.5
LOG = SCALE * 1.4426950408889634
NEG = -1e30
CHUNK = 256


def dot(a, b, dims):
    return lax.dot_general(a, b, dims, preferred_element_type=F32)


def kernel(
    tl_ref, image_qkv, text_qkv, image_grad, text_grad, image_out, text_out,
    qg_own, kv_own, qg_all, kv_all, kt_all, s_ref, p_ref, dp_ref, acc, st,
    dq_st, dkv_st, r1_q, r1_kv, r2_q, r2_kv, g_q, g_kv, f_q, f_kv,
    sent, a_r, b_r, f_r, st_r, r_r, g_r,
):
    seq = lax.axis_index("seq")
    core = lax.axis_index("head")
    y, z, x = seq // 16, lax.rem(seq // 4, 4), lax.rem(seq, 4)

    def fwd(i, r):
        return lax.rem(i + r, SIDE)

    def back(i, r):
        return lax.rem(i + SIDE - r, SIDE)

    def at_x(i):
        return (y * 16 + z * 4 + i, core)

    def at_y(i):
        return (i * 16 + z * 4 + x, core)

    def at_z(i):
        return (y * 16 + i * 4 + x, core)

    def remote(src, dst, send, recv, device):
        return pltpu.make_async_remote_copy(
            src_ref=src, dst_ref=dst, send_sem=send, recv_sem=recv,
            device_id=device, device_id_type=MESH,
        )

    others = range(1, SIDE)

    def copies_a(h, r):
        t = fwd(x, r)
        return [
            remote(qg_own.at[HG * t + h], qg_all.at[h, y, x], sent.at[0], a_r.at[h, r - 1], at_x(t)),
            remote(kv_own.at[HG * t + h], kv_all.at[h, z, x], sent.at[0], a_r.at[h, r - 1], at_x(t)),
        ]

    def arrived(ref, sem):
        remote(ref, ref, sem, sem, (seq, core)).wait_recv()

    def gone(ref, sem):
        remote(ref, ref, sem, sem, (seq, core)).wait_send()

    def copies_b(h, r):
        f = back(x, r)
        q, k = qg_all.at[h, y, f], kv_all.at[h, z, f]
        sems = (sent.at[1], b_r.at[h, r])
        return [
            remote(q, q, *sems, at_y(fwd(y, 1))),
            remote(k, k, *sems, at_z(fwd(z, 1))),
            remote(q, q, *sems, at_y(back(y, 1))),
            remote(k, k, *sems, at_z(back(z, 1))),
        ]

    def copies_f(h, r):
        come, go = (back, fwd) if r % 2 == 0 else (fwd, back)
        f = back(x, r)
        q, k = qg_all.at[h, come(y, 1), f], kv_all.at[h, come(z, 1), f]
        sems = (sent.at[2], f_r.at[h])
        return [remote(q, q, *sems, at_y(go(y, 1))), remote(k, k, *sems, at_z(go(z, 1)))]

    def copy_st(u, r):
        return remote(st.at[u, 0], st.at[u, r], sent.at[3], st_r.at[u], at_y(fwd(y, r)))

    def copies_r1(h, kv):
        src, dst, at, i = (dkv_st, r1_kv, at_z, z) if kv else (dq_st, r1_q, at_y, y)
        return [
            remote(src.at[h, fwd(i, 2), n], dst.at[h, n], sent.at[4 + kv], r_r.at[kv, h], at(t))
            for n, t in enumerate((fwd(i, 1), back(i, 1)))
        ]

    def copies_r2(h, kv):
        if not kv:
            return [
                remote(dq_st.at[h, t], r2_q.at[h, n], sent.at[6], r_r.at[2, h], at_y(t))
                for n, t in enumerate((fwd(y, 1), back(y, 1)))
            ]
        return [
            remote(dkv_st.at[h, t, i], r2_kv.at[h, n, i], sent.at[7], r_r.at[3 + i, h], at_z(t))
            for i in range(2)
            for n, t in enumerate((fwd(z, 1), back(z, 1)))
        ]

    def copy_g(h, r, kv):
        src, dst = (g_kv, f_kv) if kv else (g_q, f_q)
        t = fwd(x, r)
        return remote(src.at[h, t], dst.at[HG * x + h], sent.at[8 + kv], g_r.at[kv, h], at_x(t))

    barrier = pltpu.get_barrier_semaphore()
    for r in others:
        for place in (at_x(fwd(x, r)), at_y(fwd(y, r)), at_z(fwd(z, r))):
            pl.semaphore_signal(barrier, inc=1, device_id=place, device_id_type=MESH)

    def column(image, text, pair):
        cols = slice(pair * TOK, min((pair + 1) * TOK, image.shape[-1]))
        return jnp.concatenate([image[:, cols].astype(F32), text[:, cols].astype(F32)], 0)

    heads = image_grad.shape[1] // HEAD_DIM
    for pair in range((heads + 1) // 2):
        query, key, value = (column(image_qkv.at[i], text_qkv.at[i], pair) for i in range(3))
        grad = column(image_grad, text_grad, pair)
        for own, left, right in ((qg_own, query, grad), (kv_own, key, value)):
            own[2 * pair] = jnp.concatenate([left[:, :HEAD_DIM], right[:, :HEAD_DIM]], 1).astype(BF)
            if 2 * pair + 1 < heads:
                own[2 * pair + 1] = jnp.concatenate([left[:, HEAD_DIM:], right[:, HEAD_DIM:]], 1).astype(BF)
    for slot in range(heads, SIDE * HG):
        qg_own[slot] = jnp.zeros((TOK, TOK), BF)
        kv_own[slot] = jnp.zeros((TOK, TOK), BF)

    pl.semaphore_wait(barrier, 3 * (SIDE - 1))

    def start_a(h):
        for r in others:
            for copy in copies_a(h, r):
                copy.start()
        qg_all[h, y, x] = qg_own[HG * x + h]
        kv_all[h, z, x] = kv_own[HG * x + h]

    order = (0, 1, 3, 2)

    def spread(h):
        for r in order:
            if r:
                arrived(qg_all.at[h, 0, pl.ds(0, 2)], a_r.at[h, r - 1])
            for copy in copies_b(h, r):
                copy.start()

    def forward(h):
        for r in order:
            arrived(qg_all.at[h, 0], b_r.at[h, r])
            for copy in copies_f(h, r):
                copy.start()

    def receive(h):
        arrived(qg_all.at[h, pl.ds(0, 2)], f_r.at[h])
        for k in range(SIDE):
            kt_all[h, k] = kv_all[h, k].reshape(ROWS, TOK).T[:HEAD_DIM]

    def phase1(h, half):
        count = 2 * ROWS
        qg = qg_all[h, 2 * half : 2 * half + 2].reshape(count, TOK)
        lane = lax.broadcasted_iota(jnp.int32, qg.shape, 1)
        q0 = jnp.where(lane < HEAD_DIM, qg, jnp.zeros_like(qg))
        g0 = jnp.where(lane < HEAD_DIM, jnp.zeros_like(qg), qg)
        sub = lax.broadcasted_iota(jnp.int32, (8, count), 0)
        top = jnp.full((8, count), NEG, F32)
        for k in range(SIDE):
            s = dot(kv_all[h, k].reshape(ROWS, TOK), q0, NT)
            s_ref[k * ROWS : (k + 1) * ROWS, :] = s
            parts = s.reshape(SIDE, TOK // 8, 8, count)
            top = jnp.maximum(top, jnp.max(parts[:, : TOK // 8 - 1].reshape(-1, 8, count), axis=0))
            for i in range(SIDE):
                valid = (y * 16 + k * 4 + i) * 8 + sub < tl_ref[0]
                text = jnp.where(valid, parts[i, TOK // 8 - 1], NEG)
                end = k * ROWS + (i + 1) * TOK
                s_ref[end - 8 : end, :] = text
                top = jnp.maximum(top, text)
        top = jnp.max(top, axis=0, keepdims=True) * LOG
        total = jnp.zeros((8, count), F32)
        weighted = jnp.zeros((8, count), F32)
        for k in range(SIDE):
            rows = slice(k * ROWS, (k + 1) * ROWS)
            d = dot(kv_all[h, k].reshape(ROWS, TOK), g0, NT)
            p = jnp.exp2(s_ref[rows, :] * LOG - top)
            total += jnp.sum(p.reshape(-1, 8, count), axis=0)
            weighted += jnp.sum((p * d).reshape(-1, 8, count), axis=0)
            p_ref[half, rows, :] = p.astype(BF)
            dp_ref[half, rows, :] = d
        stats = (top, jnp.sum(total, axis=0, keepdims=True), jnp.sum(weighted, axis=0, keepdims=True))
        parts = [s[:, i * TOK : (i + 1) * TOK] for s in stats for i in range(2 * SIDE)]
        st[2 * h + half, 0] = jnp.concatenate(parts, 0)
        for r in others:
            copy_st(2 * h + half, r).start()

    def row_terms(u):
        arrived(st.at[u, pl.ds(1, SIDE - 1)], st_r.at[u])
        stats = [st[u, r] for r in range(SIDE)]
        tops = [s[0:8] for s in stats]
        top = jnp.maximum(jnp.maximum(tops[0], tops[1]), jnp.maximum(tops[2], tops[3]))
        parts = [jnp.exp2(t - top) for t in tops]
        total = sum(s[8:16] * e for s, e in zip(stats, parts))
        factors = parts[0] / total
        deltas = sum(s[16:24] * e for s, e in zip(stats, parts)) / total
        return [
            [jnp.concatenate([v[i : i + 1] for i in range(SIDE * j, SIDE * (j + 1))], 1) for v in (factors, deltas)]
            for j in range(2)
        ]

    def apart(qg):
        lane = lax.broadcasted_iota(jnp.int32, qg.shape, 1)
        zero = jnp.zeros_like(qg)
        return jnp.where(lane < HEAD_DIM, qg, zero), jnp.where(lane < HEAD_DIM, zero, qg)

    def keep_dq(h, slot, dq):
        dq = (dq * SCALE).astype(BF)
        for i in range(2):
            dq_st[h, slot, i] = dq[:, i * ROWS // 2 : (i + 1) * ROWS // 2]

    def keep_dkv(h, k, dkv):
        lane = lax.broadcasted_iota(jnp.int32, dkv.shape, 1)
        dkv = (dkv * jnp.where(lane < HEAD_DIM, SCALE, 1.0)).astype(BF)
        dkv_st[h, k] = dkv.reshape(2, ROWS // 2, TOK)

    def phase2(h, half):
        terms = row_terms(2 * h + half)
        for j in range(2):
            factor, delta = terms[j]
            q0, g0 = apart(qg_all[h, 2 * half + j].reshape(ROWS, TOK))
            cols = slice(j * ROWS, (j + 1) * ROWS)
            dq = jnp.zeros((HEAD_DIM, ROWS), F32)
            for c in range(KEYS // CHUNK):
                rows = slice(c * CHUNK, (c + 1) * CHUNK)
                p = p_ref[half, rows, cols].astype(F32) * factor
                ds = (p * (dp_ref[half, rows, cols] - delta)).astype(BF)
                part = dot(p.astype(BF), g0, NN) + dot(ds, q0, NN)
                if half == 0 and j == 0:
                    acc[rows, :] = part
                else:
                    acc[rows, :] += part
                per = ROWS // CHUNK
                at = c % per * CHUNK
                dq += dot(kt_all[h, c // per, :, at : at + CHUNK], ds, NN)
            keep_dq(h, 2 * half + j, dq)
        if half == 1:
            for k in range(SIDE):
                keep_dkv(h, k, acc[k * ROWS : (k + 1) * ROWS, :])
            for copy in copies_r1(h, 0) + copies_r1(h, 1):
                copy.start()

    def combine_q(h):
        arrived(r1_q.at[h], r_r.at[0, h])
        for n, t in enumerate((fwd(y, 1), back(y, 1))):
            dq_st[h, t, n] = (dq_st[h, t, n].astype(F32) + r1_q[h, n].astype(F32)).astype(BF)
        for copy in copies_r2(h, 0):
            copy.start()

    def combine_kv(h):
        arrived(r1_kv.at[h], r_r.at[1, h])
        for n, t in enumerate((fwd(z, 1), back(z, 1))):
            dkv_st[h, t, n] = (dkv_st[h, t, n].astype(F32) + r1_kv[h, n].astype(F32)).astype(BF)
        for copy in copies_r2(h, 1):
            copy.start()

    def last_unit():
        h = HG - 1
        terms = row_terms(2 * h + 1)
        q0, g0 = apart(qg_all[h, 2:4].reshape(2 * ROWS, TOK))

        def scores(k, dqs):
            out = []
            for j, dq in enumerate(dqs):
                factor, delta = terms[j]
                cols = slice(j * ROWS, (j + 1) * ROWS)
                for c in range(ROWS // CHUNK):
                    rows = pl.ds(pl.multiple_of(k * ROWS + c * CHUNK, CHUNK), CHUNK)
                    p = p_ref[1, rows, cols].astype(F32) * factor
                    ds = (p * (dp_ref[1, rows, cols] - delta)).astype(BF)
                    p_ref[1, rows, cols] = p.astype(BF)
                    p_ref[0, rows, cols] = ds
                    dq += dot(kt_all[h, k, :, c * CHUNK : (c + 1) * CHUNK], ds, NN)
                out.append(dq)
            return out

        def sums(k):
            rows = pl.ds(pl.multiple_of(k * ROWS, ROWS), ROWS)
            keep_dkv(h, k, acc[rows, :] + dot(p_ref[1, rows, :], g0, NN) + dot(p_ref[0, rows, :], q0, NN))

        dqs = [jnp.zeros((HEAD_DIM, ROWS), F32)] * 2
        far, near, own = fwd(z, 2), (fwd(z, 1), back(z, 1)), z
        dqs = scores(far, dqs)
        sums(far)
        for copy in copies_r1(h, 1):
            copy.start()
        for k in near + (own,):
            dqs = scores(k, dqs)
        for j in range(2):
            keep_dq(h, 2 + j, dqs[j])
        for copy in copies_r1(h, 0):
            copy.start()
        for k in near:
            sums(k)
        hand_over(HG - 2)
        combine_kv(h)
        combine_q(h)
        sums(own)

    def hand_over(h):
        arrived(r2_q.at[h], r_r.at[2, h])
        for i in range(2):
            dq = dq_st[h, y, i].astype(F32) + r2_q[h, 0, i].astype(F32) + r2_q[h, 1, i].astype(F32)
            for k in range(2):
                g_q[h, 2 * i + k] = dq[:, k * TOK : (k + 1) * TOK].astype(BF)
        for r in (2, 1, 3):
            copy_g(h, r, 0).start()
        for i in range(2):
            arrived(r2_kv.at[h, 0], r_r.at[3 + i, h])
            dkv = dkv_st[h, z, i].astype(F32) + r2_kv[h, 0, i].astype(F32) + r2_kv[h, 1, i].astype(F32)
            for k in range(2):
                g_kv[h, 2 * i + k] = dkv[k * TOK : (k + 1) * TOK, :].astype(BF)
            for r in (2, 1, 3):

                @pl.when(fwd(x, r) // 2 == i)
                def _():
                    copy_g(h, r, 1).start()

        f_q[HG * x + h] = g_q[h, x]
        f_kv[HG * x + h] = g_kv[h, x]

    start_a(0)
    spread(0)
    start_a(1)
    forward(0)

    def step(h, carry):
        receive(h)

        @pl.when(h < HG - 2)
        def _():
            start_a(h + 2)

        @pl.when((h > 0) & (h < HG - 1))
        def _():
            spread(h + 1)

        phase1(h, 0)

        @pl.when(h == 0)
        def _():
            spread(1)

        @pl.when(h > 1)
        def _():
            hand_over(h - 2)

        @pl.when(h > 0)
        def _():
            phase2(h - 1, 1)

        @pl.when((h > 0) & (h < HG - 1))
        def _():
            forward(h + 1)

        phase1(h, 1)

        @pl.when(h == 0)
        def _():
            forward(1)

        @pl.when(h > 0)
        def _():
            combine_q(h - 1)
            combine_kv(h - 1)

        phase2(h, 0)
        return carry

    lax.fori_loop(0, HG, step, 0)
    last_unit()
    hand_over(HG - 1)

    def finish(h, carry):
        arrived(g_q.at[h, pl.ds(0, SIDE - 1)], g_r.at[0, h])
        arrived(g_kv.at[h, pl.ds(0, SIDE - 1)], g_r.at[1, h])
        return carry

    lax.fori_loop(0, HG, finish, 0)
    moved = (
        qg_all.at[:, pl.ds(0, 2), pl.ds(0, SIDE - 1)],
        qg_all,
        qg_all.at[:, pl.ds(0, 2)],
        st.at[:, pl.ds(0, SIDE - 1)],
        r1_q,
        r1_kv,
        r2_q,
        r2_kv,
        g_q.at[:, pl.ds(0, SIDE - 1)],
        g_kv.at[:, pl.ds(0, SIDE - 1)],
    )
    for i, ref in enumerate(moved):
        gone(ref, sent.at[i])

    image_rows = image_grad.shape[0]
    for pair in range((heads + 1) // 2):
        both = 2 * pair + 1 < heads
        width = TOK if both else HEAD_DIM
        cols = slice(pair * TOK, pair * TOK + width)
        first, second = f_kv[2 * pair].astype(F32), f_kv[2 * pair + 1].astype(F32)
        query = jnp.concatenate([f_q[2 * pair], f_q[2 * pair + 1]], 0).astype(F32).T
        key = jnp.concatenate([first[:, :HEAD_DIM], second[:, :HEAD_DIM]], 1)
        value = jnp.concatenate([first[:, HEAD_DIM:], second[:, HEAD_DIM:]], 1)
        for i, whole in enumerate((query, key, value)):
            image_out[i, :, cols] = whole[:image_rows, :width].astype(BF)
            text_out[i, :, cols] = whole[image_rows:, :width].astype(BF)


def body(image_qkv, text_qkv, image_grad, text_grad, text_len):
    slots = SIDE * HG
    vmem = pl.BlockSpec(memory_space=pltpu.VMEM)
    return pl.pallas_call(
        kernel,
        out_shape=(
            jax.ShapeDtypeStruct(image_qkv.shape, BF),
            jax.ShapeDtypeStruct(text_qkv.shape, BF),
        ),
        in_specs=[pl.BlockSpec(memory_space=pltpu.SMEM), vmem, vmem, vmem, vmem],
        out_specs=(vmem, vmem),
        scratch_shapes=[
            pltpu.VMEM((slots, TOK, TOK), BF),
            pltpu.VMEM((slots, TOK, TOK), BF),
            pltpu.VMEM((HG, SIDE, SIDE, TOK, TOK), BF),
            pltpu.VMEM((HG, SIDE, SIDE, TOK, TOK), BF),
            pltpu.VMEM((HG, SIDE, HEAD_DIM, ROWS), BF),
            pltpu.VMEM((KEYS, 2 * ROWS), F32),
            pltpu.VMEM((2, KEYS, 2 * ROWS), BF),
            pltpu.VMEM((2, KEYS, 2 * ROWS), F32),
            pltpu.VMEM((KEYS, TOK), F32),
            pltpu.VMEM((2 * HG, SIDE, 6 * SIDE, TOK), F32),
            pltpu.VMEM((HG, SIDE, 2, HEAD_DIM, ROWS // 2), BF),
            pltpu.VMEM((HG, SIDE, 2, ROWS // 2, TOK), BF),
            pltpu.VMEM((HG, 2, HEAD_DIM, ROWS // 2), BF),
            pltpu.VMEM((HG, 2, ROWS // 2, TOK), BF),
            pltpu.VMEM((HG, 2, 2, HEAD_DIM, ROWS // 2), BF),
            pltpu.VMEM((HG, 2, 2, ROWS // 2, TOK), BF),
            pltpu.VMEM((HG, SIDE, HEAD_DIM, TOK), BF),
            pltpu.VMEM((HG, SIDE, TOK, TOK), BF),
            pltpu.VMEM((slots, HEAD_DIM, TOK), BF),
            pltpu.VMEM((slots, TOK, TOK), BF),
        ]
        + [
            pltpu.SemaphoreType.DMA(shape)
            for shape in [(10,), (HG, SIDE - 1), (HG, SIDE), (HG,), (2 * HG,), (5, HG), (2, HG)]
        ],
        compiler_params=pltpu.CompilerParams(
            collective_id=0, has_side_effects=True, vmem_limit_bytes=60 * 2**20
        ),
    )(text_len, image_qkv, text_qkv, image_grad, text_grad)


def solution(mesh):
    return jax.shard_map(
        body,
        mesh=mesh,
        in_specs=(
            P(None, "seq", "head"),
            P(None, "seq", "head"),
            P("seq", "head"),
            P("seq", "head"),
            P(),
        ),
        out_specs=(P(None, "seq", "head"), P(None, "seq", "head")),
        check_vma=False,
    )
```

```python
import jax
import jax.numpy as jnp
from jax import lax
from jax.experimental import pallas as pl
from jax.experimental.pallas import tpu as pltpu
from jax.sharding import PartitionSpec as P

F32 = jnp.float32
BF = jnp.bfloat16
MESH = pl.DeviceIdType.MESH
NT = (((1,), (1,)), ((), ()))
NN = (((1,), (0,)), ((), ()))
HEAD_DIM = 64
SIDE = 4
HG = 5
TOK = 128
ROWS = SIDE * TOK
KEYS = SIDE * ROWS
SCALE = HEAD_DIM**-0.5
LOG = SCALE * 1.4426950408889634
NEG = -1e30
CHUNK = 256


def dot(a, b, dims):
    return lax.dot_general(a, b, dims, preferred_element_type=F32)


def kernel(
    tl_ref, image_qkv, text_qkv, image_grad, text_grad, image_out, text_out,
    qg_own, kv_own, qg_all, kv_all, kt_all, s_ref, p_ref, dp_ref, acc, st,
    dq_st, dkv_st, r1_q, r1_kv, r2_q, r2_kv, g_q, g_kv, f_q, f_kv,
    sent, a_r, b_r, f_r, st_r, r_r, g_r,
):
    seq = lax.axis_index("seq")
    core = lax.axis_index("head")
    y, z, x = seq // 16, lax.rem(seq // 4, 4), lax.rem(seq, 4)

    def fwd(i, r):
        return lax.rem(i + r, SIDE)

    def back(i, r):
        return lax.rem(i + SIDE - r, SIDE)

    def at_x(i):
        return (y * 16 + z * 4 + i, core)

    def at_y(i):
        return (i * 16 + z * 4 + x, core)

    def at_z(i):
        return (y * 16 + i * 4 + x, core)

    def remote(src, dst, send, recv, device):
        return pltpu.make_async_remote_copy(
            src_ref=src, dst_ref=dst, send_sem=send, recv_sem=recv,
            device_id=device, device_id_type=MESH,
        )

    others = range(1, SIDE)

    def copies_a(h, r):
        t = fwd(x, r)
        return [
            remote(qg_own.at[HG * t + h], qg_all.at[h, y, x], sent.at[0], a_r.at[h, r - 1], at_x(t)),
            remote(kv_own.at[HG * t + h], kv_all.at[h, z, x], sent.at[0], a_r.at[h, r - 1], at_x(t)),
        ]

    def arrived(ref, sem):
        remote(ref, ref, sem, sem, (seq, core)).wait_recv()

    def gone(ref, sem):
        remote(ref, ref, sem, sem, (seq, core)).wait_send()

    def copies_b(h, r):
        f = back(x, r)
        q, k = qg_all.at[h, y, f], kv_all.at[h, z, f]
        sems = (sent.at[1], b_r.at[h, r])
        return [
            remote(q, q, *sems, at_y(fwd(y, 1))),
            remote(k, k, *sems, at_z(fwd(z, 1))),
            remote(q, q, *sems, at_y(back(y, 1))),
            remote(k, k, *sems, at_z(back(z, 1))),
        ]

    def copies_f(h, r):
        come, go = (back, fwd) if r % 2 == 0 else (fwd, back)
        f = back(x, r)
        q, k = qg_all.at[h, come(y, 1), f], kv_all.at[h, come(z, 1), f]
        sems = (sent.at[2], f_r.at[h])
        return [remote(q, q, *sems, at_y(go(y, 1))), remote(k, k, *sems, at_z(go(z, 1)))]

    def copy_st(u, r):
        return remote(st.at[u, 0], st.at[u, r], sent.at[3], st_r.at[u], at_y(fwd(y, r)))

    def copies_r1(h, kv):
        src, dst, at, i = (dkv_st, r1_kv, at_z, z) if kv else (dq_st, r1_q, at_y, y)
        return [
            remote(src.at[h, fwd(i, 2), n], dst.at[h, n], sent.at[4 + kv], r_r.at[kv, h], at(t))
            for n, t in enumerate((fwd(i, 1), back(i, 1)))
        ]

    def copies_r2(h, kv):
        if not kv:
            return [
                remote(dq_st.at[h, t], r2_q.at[h, n], sent.at[6], r_r.at[2, h], at_y(t))
                for n, t in enumerate((fwd(y, 1), back(y, 1)))
            ]
        return [
            remote(dkv_st.at[h, t, i], r2_kv.at[h, n, i], sent.at[7], r_r.at[3 + i, h], at_z(t))
            for i in range(2)
            for n, t in enumerate((fwd(z, 1), back(z, 1)))
        ]

    def copy_g(h, r, kv):
        src, dst = (g_kv, f_kv) if kv else (g_q, f_q)
        t = fwd(x, r)
        return remote(src.at[h, t], dst.at[HG * x + h], sent.at[8 + kv], g_r.at[kv, h], at_x(t))

    barrier = pltpu.get_barrier_semaphore()
    for r in others:
        for place in (at_x(fwd(x, r)), at_y(fwd(y, r)), at_z(fwd(z, r))):
            pl.semaphore_signal(barrier, inc=1, device_id=place, device_id_type=MESH)

    def column(image, text, pair):
        cols = slice(pair * TOK, min((pair + 1) * TOK, image.shape[-1]))
        return jnp.concatenate([image[:, cols].astype(F32), text[:, cols].astype(F32)], 0)

    heads = image_grad.shape[1] // HEAD_DIM
    for pair in range((heads + 1) // 2):
        query, key, value = (column(image_qkv.at[i], text_qkv.at[i], pair) for i in range(3))
        grad = column(image_grad, text_grad, pair)
        for own, left, right in ((qg_own, query, grad), (kv_own, key, value)):
            own[2 * pair] = jnp.concatenate([left[:, :HEAD_DIM], right[:, :HEAD_DIM]], 1).astype(BF)
            if 2 * pair + 1 < heads:
                own[2 * pair + 1] = jnp.concatenate([left[:, HEAD_DIM:], right[:, HEAD_DIM:]], 1).astype(BF)
    for slot in range(heads, SIDE * HG):
        qg_own[slot] = jnp.zeros((TOK, TOK), BF)
        kv_own[slot] = jnp.zeros((TOK, TOK), BF)

    pl.semaphore_wait(barrier, 3 * (SIDE - 1))

    def start_a(h):
        for r in others:
            for copy in copies_a(h, r):
                copy.start()
        qg_all[h, y, x] = qg_own[HG * x + h]
        kv_all[h, z, x] = kv_own[HG * x + h]

    order = (0, 1, 3, 2)

    def spread(h):
        for r in order:
            if r:
                arrived(qg_all.at[h, 0, pl.ds(0, 2)], a_r.at[h, r - 1])
            for copy in copies_b(h, r):
                copy.start()

    def forward(h):
        for r in order:
            arrived(qg_all.at[h, 0], b_r.at[h, r])
            for copy in copies_f(h, r):
                copy.start()

    def receive(h):
        arrived(qg_all.at[h, pl.ds(0, 2)], f_r.at[h])
        for k in range(SIDE):
            kt_all[h, k] = kv_all[h, k].reshape(ROWS, TOK).T[:HEAD_DIM]

    def phase1(h, half):
        count = 2 * ROWS
        qg = qg_all[h, 2 * half : 2 * half + 2].reshape(count, TOK)
        lane = lax.broadcasted_iota(jnp.int32, qg.shape, 1)
        q0 = jnp.where(lane < HEAD_DIM, qg, jnp.zeros_like(qg))
        g0 = jnp.where(lane < HEAD_DIM, jnp.zeros_like(qg), qg)
        sub = lax.broadcasted_iota(jnp.int32, (8, count), 0)
        top = jnp.full((8, count), NEG, F32)
        for k in range(SIDE):
            s = dot(kv_all[h, k].reshape(ROWS, TOK), q0, NT)
            s_ref[k * ROWS : (k + 1) * ROWS, :] = s
            parts = s.reshape(SIDE, TOK // 8, 8, count)
            top = jnp.maximum(top, jnp.max(parts[:, : TOK // 8 - 1].reshape(-1, 8, count), axis=0))
            for i in range(SIDE):
                valid = (y * 16 + k * 4 + i) * 8 + sub < tl_ref[0]
                text = jnp.where(valid, parts[i, TOK // 8 - 1], NEG)
                end = k * ROWS + (i + 1) * TOK
                s_ref[end - 8 : end, :] = text
                top = jnp.maximum(top, text)
        top = jnp.max(top, axis=0, keepdims=True) * LOG
        total = jnp.zeros((8, count), F32)
        weighted = jnp.zeros((8, count), F32)
        for k in range(SIDE):
            rows = slice(k * ROWS, (k + 1) * ROWS)
            d = dot(kv_all[h, k].reshape(ROWS, TOK), g0, NT)
            p = jnp.exp2(s_ref[rows, :] * LOG - top)
            total += jnp.sum(p.reshape(-1, 8, count), axis=0)
            weighted += jnp.sum((p * d).reshape(-1, 8, count), axis=0)
            p_ref[half, rows, :] = p.astype(BF)
            dp_ref[half, rows, :] = d
        stats = (top, jnp.sum(total, axis=0, keepdims=True), jnp.sum(weighted, axis=0, keepdims=True))
        parts = [s[:, i * TOK : (i + 1) * TOK] for s in stats for i in range(2 * SIDE)]
        st[2 * h + half, 0] = jnp.concatenate(parts, 0)
        for r in others:
            copy_st(2 * h + half, r).start()

    def row_terms(u):
        arrived(st.at[u, pl.ds(1, SIDE - 1)], st_r.at[u])
        stats = [st[u, r] for r in range(SIDE)]
        tops = [s[0:8] for s in stats]
        top = jnp.maximum(jnp.maximum(tops[0], tops[1]), jnp.maximum(tops[2], tops[3]))
        parts = [jnp.exp2(t - top) for t in tops]
        total = sum(s[8:16] * e for s, e in zip(stats, parts))
        factors = parts[0] / total
        deltas = sum(s[16:24] * e for s, e in zip(stats, parts)) / total
        return [
            [jnp.concatenate([v[i : i + 1] for i in range(SIDE * j, SIDE * (j + 1))], 1) for v in (factors, deltas)]
            for j in range(2)
        ]

    def apart(qg):
        lane = lax.broadcasted_iota(jnp.int32, qg.shape, 1)
        zero = jnp.zeros_like(qg)
        return jnp.where(lane < HEAD_DIM, qg, zero), jnp.where(lane < HEAD_DIM, zero, qg)

    def keep_dq(h, slot, dq):
        dq = (dq * SCALE).astype(BF)
        for i in range(2):
            dq_st[h, slot, i] = dq[:, i * ROWS // 2 : (i + 1) * ROWS // 2]

    def keep_dkv(h, k, dkv):
        lane = lax.broadcasted_iota(jnp.int32, dkv.shape, 1)
        dkv = (dkv * jnp.where(lane < HEAD_DIM, SCALE, 1.0)).astype(BF)
        dkv_st[h, k] = dkv.reshape(2, ROWS // 2, TOK)

    def phase2(h, half):
        terms = row_terms(2 * h + half)
        for j in range(2):
            factor, delta = terms[j]
            q0, g0 = apart(qg_all[h, 2 * half + j].reshape(ROWS, TOK))
            cols = slice(j * ROWS, (j + 1) * ROWS)
            dq = jnp.zeros((HEAD_DIM, ROWS), F32)
            for c in range(KEYS // CHUNK):
                rows = slice(c * CHUNK, (c + 1) * CHUNK)
                p = p_ref[half, rows, cols].astype(F32) * factor
                ds = (p * (dp_ref[half, rows, cols] - delta)).astype(BF)
                part = dot(p.astype(BF), g0, NN) + dot(ds, q0, NN)
                if half == 0 and j == 0:
                    acc[rows, :] = part
                else:
                    acc[rows, :] += part
                per = ROWS // CHUNK
                at = c % per * CHUNK
                dq += dot(kt_all[h, c // per, :, at : at + CHUNK], ds, NN)
            keep_dq(h, 2 * half + j, dq)
        if half == 1:
            for k in range(SIDE):
                keep_dkv(h, k, acc[k * ROWS : (k + 1) * ROWS, :])
            for copy in copies_r1(h, 0) + copies_r1(h, 1):
                copy.start()

    def combine_q(h):
        arrived(r1_q.at[h], r_r.at[0, h])
        for n, t in enumerate((fwd(y, 1), back(y, 1))):
            dq_st[h, t, n] = (dq_st[h, t, n].astype(F32) + r1_q[h, n].astype(F32)).astype(BF)
        for copy in copies_r2(h, 0):
            copy.start()

    def combine_kv(h):
        arrived(r1_kv.at[h], r_r.at[1, h])
        for n, t in enumerate((fwd(z, 1), back(z, 1))):
            dkv_st[h, t, n] = (dkv_st[h, t, n].astype(F32) + r1_kv[h, n].astype(F32)).astype(BF)
        for copy in copies_r2(h, 1):
            copy.start()

    def last_unit():
        h = HG - 1
        terms = row_terms(2 * h + 1)
        q0, g0 = apart(qg_all[h, 2:4].reshape(2 * ROWS, TOK))

        def scores(k, dqs):
            out = []
            for j, dq in enumerate(dqs):
                factor, delta = terms[j]
                cols = slice(j * ROWS, (j + 1) * ROWS)
                for c in range(ROWS // CHUNK):
                    rows = pl.ds(pl.multiple_of(k * ROWS + c * CHUNK, CHUNK), CHUNK)
                    p = p_ref[1, rows, cols].astype(F32) * factor
                    ds = (p * (dp_ref[1, rows, cols] - delta)).astype(BF)
                    p_ref[1, rows, cols] = p.astype(BF)
                    p_ref[0, rows, cols] = ds
                    dq += dot(kt_all[h, k, :, c * CHUNK : (c + 1) * CHUNK], ds, NN)
                out.append(dq)
            return out

        def sums(k):
            rows = pl.ds(pl.multiple_of(k * ROWS, ROWS), ROWS)
            keep_dkv(h, k, acc[rows, :] + dot(p_ref[1, rows, :], g0, NN) + dot(p_ref[0, rows, :], q0, NN))

        dqs = [jnp.zeros((HEAD_DIM, ROWS), F32)] * 2
        far, near, own = fwd(z, 2), (fwd(z, 1), back(z, 1)), z
        dqs = scores(far, dqs)
        sums(far)
        for copy in copies_r1(h, 1):
            copy.start()
        for k in near + (own,):
            dqs = scores(k, dqs)
        for j in range(2):
            keep_dq(h, 2 + j, dqs[j])
        for copy in copies_r1(h, 0):
            copy.start()
        for k in near:
            sums(k)
        hand_over(HG - 2)
        combine_kv(h)
        combine_q(h)
        sums(own)

    def hand_over(h):
        arrived(r2_q.at[h], r_r.at[2, h])
        for i in range(2):
            dq = dq_st[h, y, i].astype(F32) + r2_q[h, 0, i].astype(F32) + r2_q[h, 1, i].astype(F32)
            for k in range(2):
                g_q[h, 2 * i + k] = dq[:, k * TOK : (k + 1) * TOK].astype(BF)
        for r in (2, 1, 3):
            copy_g(h, r, 0).start()
        for i in range(2):
            arrived(r2_kv.at[h, 0], r_r.at[3 + i, h])
            dkv = dkv_st[h, z, i].astype(F32) + r2_kv[h, 0, i].astype(F32) + r2_kv[h, 1, i].astype(F32)
            for k in range(2):
                g_kv[h, 2 * i + k] = dkv[k * TOK : (k + 1) * TOK, :].astype(BF)
            for r in (2, 1, 3):

                @pl.when(fwd(x, r) // 2 == i)
                def _():
                    copy_g(h, r, 1).start()

        f_q[HG * x + h] = g_q[h, x]
        f_kv[HG * x + h] = g_kv[h, x]

    start_a(0)
    spread(0)
    start_a(1)
    forward(0)

    def step(h, carry):
        receive(h)

        @pl.when(h < HG - 2)
        def _():
            start_a(h + 2)

        @pl.when((h > 0) & (h < HG - 1))
        def _():
            spread(h + 1)

        phase1(h, 0)

        @pl.when(h == 0)
        def _():
            spread(1)

        @pl.when(h > 1)
        def _():
            hand_over(h - 2)

        @pl.when(h > 0)
        def _():
            phase2(h - 1, 1)

        @pl.when((h > 0) & (h < HG - 1))
        def _():
            forward(h + 1)

        phase1(h, 1)

        @pl.when(h == 0)
        def _():
            forward(1)

        @pl.when(h > 0)
        def _():
            combine_q(h - 1)
            combine_kv(h - 1)

        phase2(h, 0)
        return carry

    image_rows = image_grad.shape[0]

    def assemble(some):
        for pair in some:
            both = 2 * pair + 1 < heads
            width = TOK if both else HEAD_DIM
            cols = slice(pair * TOK, pair * TOK + width)
            first, second = f_kv[2 * pair].astype(F32), f_kv[2 * pair + 1].astype(F32)
            query = jnp.concatenate([f_q[2 * pair], f_q[2 * pair + 1]], 0).astype(F32).T
            key = jnp.concatenate([first[:, :HEAD_DIM], second[:, :HEAD_DIM]], 1)
            value = jnp.concatenate([first[:, HEAD_DIM:], second[:, HEAD_DIM:]], 1)
            for i, whole in enumerate((query, key, value)):
                image_out[i, :, cols] = whole[:image_rows, :width].astype(BF)
                text_out[i, :, cols] = whole[image_rows:, :width].astype(BF)

    def finish(h, carry):
        arrived(g_q.at[h, pl.ds(0, SIDE - 1)], g_r.at[0, h])
        arrived(g_kv.at[h, pl.ds(0, SIDE - 1)], g_r.at[1, h])
        return carry

    pairs = range((heads + 1) // 2)
    late = {(HG * g + HG - 1) // 2 for g in range(SIDE)}
    lax.fori_loop(0, HG, step, 0)
    last_unit()
    lax.fori_loop(0, HG - 1, finish, 0)
    assemble(pair for pair in pairs if pair not in late)
    hand_over(HG - 1)
    finish(HG - 1, 0)
    moved = (
        qg_all.at[:, pl.ds(0, 2), pl.ds(0, SIDE - 1)],
        qg_all,
        qg_all.at[:, pl.ds(0, 2)],
        st.at[:, pl.ds(0, SIDE - 1)],
        r1_q,
        r1_kv,
        r2_q,
        r2_kv,
        g_q.at[:, pl.ds(0, SIDE - 1)],
        g_kv.at[:, pl.ds(0, SIDE - 1)],
    )
    for i, ref in enumerate(moved):
        gone(ref, sent.at[i])

    assemble(pair for pair in pairs if pair in late)


def body(image_qkv, text_qkv, image_grad, text_grad, text_len):
    slots = SIDE * HG
    vmem = pl.BlockSpec(memory_space=pltpu.VMEM)
    return pl.pallas_call(
        kernel,
        out_shape=(
            jax.ShapeDtypeStruct(image_qkv.shape, BF),
            jax.ShapeDtypeStruct(text_qkv.shape, BF),
        ),
        in_specs=[pl.BlockSpec(memory_space=pltpu.SMEM), vmem, vmem, vmem, vmem],
        out_specs=(vmem, vmem),
        scratch_shapes=[
            pltpu.VMEM((slots, TOK, TOK), BF),
            pltpu.VMEM((slots, TOK, TOK), BF),
            pltpu.VMEM((HG, SIDE, SIDE, TOK, TOK), BF),
            pltpu.VMEM((HG, SIDE, SIDE, TOK, TOK), BF),
            pltpu.VMEM((HG, SIDE, HEAD_DIM, ROWS), BF),
            pltpu.VMEM((KEYS, 2 * ROWS), F32),
            pltpu.VMEM((2, KEYS, 2 * ROWS), BF),
            pltpu.VMEM((2, KEYS, 2 * ROWS), F32),
            pltpu.VMEM((KEYS, TOK), F32),
            pltpu.VMEM((2 * HG, SIDE, 6 * SIDE, TOK), F32),
            pltpu.VMEM((HG, SIDE, 2, HEAD_DIM, ROWS // 2), BF),
            pltpu.VMEM((HG, SIDE, 2, ROWS // 2, TOK), BF),
            pltpu.VMEM((HG, 2, HEAD_DIM, ROWS // 2), BF),
            pltpu.VMEM((HG, 2, ROWS // 2, TOK), BF),
            pltpu.VMEM((HG, 2, 2, HEAD_DIM, ROWS // 2), BF),
            pltpu.VMEM((HG, 2, 2, ROWS // 2, TOK), BF),
            pltpu.VMEM((HG, SIDE, HEAD_DIM, TOK), BF),
            pltpu.VMEM((HG, SIDE, TOK, TOK), BF),
            pltpu.VMEM((slots, HEAD_DIM, TOK), BF),
            pltpu.VMEM((slots, TOK, TOK), BF),
        ]
        + [
            pltpu.SemaphoreType.DMA(shape)
            for shape in [(10,), (HG, SIDE - 1), (HG, SIDE), (HG,), (2 * HG,), (5, HG), (2, HG)]
        ],
        compiler_params=pltpu.CompilerParams(
            collective_id=0, has_side_effects=True, vmem_limit_bytes=60 * 2**20
        ),
    )(text_len, image_qkv, text_qkv, image_grad, text_grad)


def solution(mesh):
    return jax.shard_map(
        body,
        mesh=mesh,
        in_specs=(
            P(None, "seq", "head"),
            P(None, "seq", "head"),
            P("seq", "head"),
            P("seq", "head"),
            P(),
        ),
        out_specs=(P(None, "seq", "head"), P(None, "seq", "head")),
        check_vma=False,
    )
```
